256 devices in a mesh: frame: 4 (over x_lo, core), height: 8 (over z), width: 8 (over x_hi, y).
Axes of the slice: x: 4 (x_hi: 2, x_lo: 2; x = x_hi * 2 + x_lo), y: 4, z: 8, core: 2. Of those that a mesh axis runs over, the one named last changes fastest.
Arguments:
- queries: bfloat16 [16, 48, 64, 128], P('frame', 'height', 'width'), may hold values from -8 to 8
- key_vectors: bfloat16 [16, 48, 64, 128], P('frame', 'height', 'width'), may hold values from -8 to 8
- value_vectors: bfloat16 [16, 48, 64, 128], P('frame', 'height', 'width'), may hold values from -24 to 24
- out_weight: bfloat16 [128, 3072], replicated, may hold values from -0.5 to 0.5
- projected_grad: bfloat16 [16, 48, 64, 3072], P('frame', 'height', 'width'), may hold values from -6 to 6
Outputs:
- projected: bfloat16 [16, 48, 64, 3072], P('frame', 'height', 'width')
- grad_query: bfloat16 [16, 48, 64, 128], P('frame', 'height', 'width')
- grad_key: bfloat16 [16, 48, 64, 128], P('frame', 'height', 'width')
- grad_value: bfloat16 [16, 48, 64, 128], P('frame', 'height', 'width')
- grad_out_weight: float32 [128, 3072], replicated
The draws below stay inside these ranges and needn't reach their ends.
All inputs are finite; a program needn't handle non-finite values.
Results may differ from the reference program's by a relative error of at most 0.023.
Values may be sent and summed in bfloat16 or wider, within the bound.
A program may use at most 128 MiB of HBM per device.

```python
import math
import jax
import jax.numpy as jnp
from jax import lax

TILE_F = 4
TILE_H = 6
TILE_W = 8
HEAD_DIM = 128
MODEL_DIM = 3072
FRAMES = 16
HEIGHT = 48
WIDTH = 64
N_FRAME = 4
N_HEIGHT = 8
N_WIDTH = 8


def draw_queries(key, part):
    own_key = jax.random.fold_in(key, 11)
    return jnp.clip(1.5 * jax.random.normal(own_key, (FRAMES, HEIGHT, WIDTH, HEAD_DIM), jnp.float32), -8.0, 8.0).astype(jnp.bfloat16)


def draw_key_vectors(key, part):
    own_key = jax.random.fold_in(key, 23)
    return jnp.clip(1.5 * jax.random.normal(own_key, (FRAMES, HEIGHT, WIDTH, HEAD_DIM), jnp.float32), -8.0, 8.0).astype(jnp.bfloat16)


def block_levels(stream_key, dims, cuts, smallest, high):
    def one(dim, shards_of):
        steps = jax.random.uniform(jax.random.fold_in(jax.random.fold_in(stream_key, 6), dim), (shards_of,), jnp.float32, smallest / len(cuts), high / len(cuts))
        return jnp.repeat(jnp.exp(steps), dims[dim] // shards_of).reshape((-1,) + (1,) * (len(dims) - dim - 1))

    factor_of = one(*cuts[0])
    for cut in cuts[1:]:
        factor_of = factor_of * one(*cut)
    return factor_of


def scatter_about(stream_key, dims, scale, reach, cuts=(), kind=jnp.bfloat16):
    level = block_levels(stream_key, dims, cuts, -0.22, 0.18) if cuts else 1.0
    drawn = jax.random.normal(stream_key, dims, jnp.float32) * scale * level
    return jnp.minimum(jnp.maximum(drawn, -reach), reach).astype(kind)


def setup_inputs(seed: int = 0) -> dict:
    seeds = jax.random.split(jax.random.key(seed), 6)
    queries = draw_queries(jax.random.fold_in(seeds[5], 71), 0)
    key_vectors = draw_key_vectors(jax.random.fold_in(seeds[5], 71), 0)
    value_vectors = scatter_about(seeds[2], (FRAMES, HEIGHT, WIDTH, HEAD_DIM), 4.0, 24.0, ((0, 4), (1, 8), (2, 8)))
    out_weight = scatter_about(seeds[3], (HEAD_DIM, MODEL_DIM), HEAD_DIM ** -0.5, 0.5)
    projected_grad = scatter_about(seeds[4], (FRAMES, HEIGHT, WIDTH, MODEL_DIM), 1.0, 6.0, ((0, 4), (1, 8), (2, 8)))
    return dict(queries=queries, key_vectors=key_vectors, value_vectors=value_vectors, out_weight=out_weight, projected_grad=projected_grad)


def window_start(position, extent):
    return jnp.maximum(jnp.minimum(position - 1, extent - 3), 0)

def to_bfloat(value):
    return lax.optimization_barrier(value.astype(jnp.bfloat16)).astype(jnp.float32)

def product(left, right):
    return jnp.dot(left, right, precision=lax.Precision.HIGHEST, preferred_element_type=jnp.float32)

def tiles_to_grid(tiled, last_dim):
    shaped = tiled.reshape(N_FRAME, N_HEIGHT, N_WIDTH, TILE_F, TILE_H, TILE_W, last_dim)
    return shaped.transpose(0, 3, 1, 4, 2, 5, 6).reshape(FRAMES, HEIGHT, WIDTH, last_dim)

def reference(queries, key_vectors, value_vectors, out_weight, projected_grad):
    inv_root = 1.0 / math.sqrt(HEAD_DIM)
    frame_span = min(3, N_FRAME)
    height_span = min(3, N_HEIGHT)
    width_span = min(3, N_WIDTH)
    key_shape = (frame_span * TILE_F, height_span * TILE_H, width_span * TILE_W, HEAD_DIM)
    tile_shape = (TILE_F, TILE_H, TILE_W)
    weight_full = out_weight.astype(jnp.float32)
    anchor = jnp.zeros((), jnp.int32)

    def one_tile(accumulators, tile_flat):
        key_acc, value_acc, weight_acc = accumulators
        frame_tile = tile_flat // (N_HEIGHT * N_WIDTH)
        height_tile = tile_flat // N_WIDTH % N_HEIGHT
        width_tile = tile_flat % N_WIDTH
        corner = (frame_tile * TILE_F, height_tile * TILE_H, width_tile * TILE_W, anchor)
        window_corner = (window_start(frame_tile, N_FRAME) * TILE_F, window_start(height_tile, N_HEIGHT) * TILE_H, window_start(width_tile, N_WIDTH) * TILE_W, anchor)
        query_rows = lax.dynamic_slice(queries, corner, tile_shape + (HEAD_DIM,)).reshape(-1, HEAD_DIM).astype(jnp.float32)
        key_rows = lax.dynamic_slice(key_vectors, window_corner, key_shape).reshape(-1, HEAD_DIM).astype(jnp.float32)
        value_rows = lax.dynamic_slice(value_vectors, window_corner, key_shape).reshape(-1, HEAD_DIM).astype(jnp.float32)
        grad_rows = lax.dynamic_slice(projected_grad, corner, tile_shape + (MODEL_DIM,)).reshape(-1, MODEL_DIM).astype(jnp.float32)
        scores = product(query_rows, key_rows.T) * inv_root
        row_max = lax.optimization_barrier(jnp.max(scores, axis=1, keepdims=True))
        row_sum = lax.optimization_barrier(jnp.sum(jnp.exp(scores - row_max), axis=1, keepdims=True))
        probability = jnp.exp(scores - row_max) / row_sum
        prob_bf = to_bfloat(probability)
        attended = to_bfloat(product(prob_bf, value_rows))
        projected_tile = product(attended, weight_full).astype(jnp.bfloat16).reshape(tile_shape + (MODEL_DIM,))
        attended_grad = to_bfloat(product(grad_rows, weight_full.T))
        weight_acc = weight_acc + product(attended.T, grad_rows)
        row_dot = lax.optimization_barrier(jnp.sum(attended_grad * attended, axis=1, keepdims=True))
        prob_grad = product(attended_grad, value_rows.T)
        score_grad = to_bfloat(probability * (prob_grad - row_dot))
        query_tile = (product(score_grad, key_rows) * inv_root).astype(jnp.bfloat16).reshape(tile_shape + (HEAD_DIM,))
        key_part = product(score_grad.T, query_rows) * inv_root
        value_part = product(prob_bf.T, attended_grad)
        key_acc = lax.dynamic_update_slice(key_acc, lax.dynamic_slice(key_acc, window_corner, key_shape) + key_part.reshape(key_shape), window_corner)
        value_acc = lax.dynamic_update_slice(value_acc, lax.dynamic_slice(value_acc, window_corner, key_shape) + value_part.reshape(key_shape), window_corner)
        return ((key_acc, value_acc, weight_acc), (projected_tile, query_tile))
    initial = (jnp.zeros((FRAMES, HEIGHT, WIDTH, HEAD_DIM), jnp.float32), jnp.zeros((FRAMES, HEIGHT, WIDTH, HEAD_DIM), jnp.float32), jnp.zeros((HEAD_DIM, MODEL_DIM), jnp.float32))
    tile_total = N_FRAME * N_HEIGHT * N_WIDTH
    finals, outputs = lax.scan(one_tile, initial, jnp.arange(tile_total, dtype=jnp.int32))
    projected = tiles_to_grid(outputs[0], MODEL_DIM)
    grad_query = tiles_to_grid(outputs[1], HEAD_DIM)
    grad_out_weight = finals[2] / float(tile_total)
    return (projected, grad_query, finals[0].astype(jnp.bfloat16), finals[1].astype(jnp.bfloat16), grad_out_weight)
```

```python
import functools
import math

import jax
import jax.experimental.pallas as pl
import jax.experimental.pallas.tpu as pltpu
import jax.numpy as jnp
from jax import lax
from jax.sharding import PartitionSpec as P

MESH = pl.DeviceIdType.MESH
ROWS = 192
DIM = 128
LIMIT = 56 * 2**20


class Place:
    def __init__(self):
        self.f = lax.axis_index("frame")
        self.h = lax.axis_index("height")
        self.w = lax.axis_index("width")
        self.xlo = self.f // 2
        self.core = self.f - 2 * self.xlo
        self.xhi = self.w // 4
        self.y = self.w - 4 * self.xhi
        self.ring = (2 * self.xhi + self.xlo) * 4 + self.y
        self.sibling = (self.xlo * 2 + 1 - self.core, self.h, self.w)
        self.partner = ((1 - self.xlo) * 2 + self.core, self.h, self.w)
        self.own_plane = self.f - self.xlo
        self.sib_plane = self.xlo * 2 + 1 - self.core - self.xlo
        self.third_plane = 2 * (1 - self.xlo)
        self.collects = self.core == self.xlo
        self.supplies = self.core != self.xlo
        self.hslot = self.h - start(self.h)
        self.wslot = self.w - start(self.w)

    def plane_chip(self, index):
        x = index // 4
        y = index - 4 * x
        xhi = x // 2
        return ((x - 2 * xhi) * 2 + self.core, self.h, xhi * 4 + y)


def start(index):
    return jnp.maximum(jnp.minimum(index - 1, 5), 0)


def neighbours(index):
    return (
        (index >= 1, index - 1),
        (index <= 6, index + 1),
        ((index == 2) | (index == 5), 7 * (index // 5)),
    )


def owners(index):
    return (
        (index >= 1, index - 1),
        (index <= 6, index + 1),
        ((index == 0) | (index == 7), 2 + 3 * (index // 7)),
    )


def remote(src, dst, send_sem, recv_sem, target):
    return pltpu.make_async_remote_copy(
        src_ref=src,
        dst_ref=dst,
        send_sem=send_sem,
        recv_sem=recv_sem,
        device_id=target,
        device_id_type=MESH,
    )


def arrived(ref, sem):
    pltpu.make_async_copy(ref, ref, sem).wait()


def greet_plane(place, barrier):
    def one(k, carry):
        target = place.plane_chip(lax.rem(place.ring + k, 16))
        pl.semaphore_signal(barrier, inc=1, device_id=target, device_id_type=MESH)
        return carry

    lax.fori_loop(1, 16, one, 0)


def greet_column(place, barrier):
    def one(k, carry):
        target = (place.f, lax.rem(place.h + k, 8), place.w)
        pl.semaphore_signal(barrier, inc=1, device_id=target, device_id_type=MESH)
        return carry

    lax.fori_loop(1, 8, one, 0)


def greet_all(place):
    barrier = pltpu.get_barrier_semaphore()
    pl.semaphore_signal(barrier, inc=1, device_id=place.sibling, device_id_type=MESH)
    greet_plane(place, barrier)
    greet_column(place, barrier)
    pl.semaphore_wait(barrier, 23)


def gather_kernel(k_ref, v_ref, kv, hsend, wsend, ssend, tsend, xsend, recv):
    place = Place()
    greet_all(place)
    own = place.own_plane * 9
    third = place.third_plane * 9

    kv[own + place.wslot * 3 + place.hslot, 0] = k_ref[...]
    kv[own + place.wslot * 3 + place.hslot, 1] = v_ref[...]

    def along_height():
        slot = own + place.wslot * 3 + place.hslot
        for i, (there, h) in enumerate(neighbours(place.h)):
            to = own + place.wslot * 3 + place.h - start(h)
            yield there, remote(
                kv.at[slot], kv.at[to], hsend.at[i], recv.at[to], (place.f, h, place.w)
            )

    def along_width(hslot):
        slot = own + place.wslot * 3 + hslot
        for i, (there, w) in enumerate(neighbours(place.w)):
            to = own + (place.w - start(w)) * 3 + hslot
            yield there, remote(
                kv.at[slot], kv.at[to], wsend.at[i, hslot], recv.at[to], (place.f, place.h, w)
            )

    def along_frame(tile):
        slot = own + tile
        to = 18 * place.xlo + tile
        yield True, remote(kv.at[slot], kv.at[slot], ssend.at[tile], recv.at[slot], place.sibling)
        yield (
            place.supplies,
            remote(kv.at[slot], kv.at[to], xsend.at[tile], recv.at[to], place.partner),
        )

    def third_on(tile):
        slot = third + tile
        yield (
            place.collects,
            remote(kv.at[slot], kv.at[slot], tsend.at[tile], recv.at[slot], place.sibling),
        )

    def begin(copies):
        for there, copy in copies:
            if there is True:
                copy.start()
            else:
                pl.when(there)(copy.start)

    def finish(copies):
        for there, copy in copies:
            if there is True:
                copy.wait_send()
            else:
                pl.when(there)(copy.wait_send)

    hslots = (place.hslot, lax.rem(place.hslot + 1, 3), lax.rem(place.hslot + 2, 3))
    wslots = (place.wslot, lax.rem(place.wslot + 1, 3), lax.rem(place.wslot + 2, 3))
    begin(along_height())
    begin(along_width(hslots[0]))
    begin(along_frame(wslots[0] * 3 + hslots[0]))
    for hslot in hslots[1:]:
        slot = own + wslots[0] * 3 + hslot
        arrived(kv.at[slot], recv.at[slot])
        begin(along_width(hslot))
        begin(along_frame(wslots[0] * 3 + hslot))
    for hslot in hslots:
        for wslot in wslots[1:]:
            slot = own + wslot * 3 + hslot
            arrived(kv.at[slot], recv.at[slot])
            begin(along_frame(wslot * 3 + hslot))
    for wslot in wslots:
        for hslot in hslots:
            slot = third + wslot * 3 + hslot
            arrived(kv.at[slot], recv.at[slot])
            begin(third_on(wslot * 3 + hslot))

    def from_sibling(tile, carry):
        slot = place.sib_plane * 9 + tile
        arrived(kv.at[slot], recv.at[slot])
        finish(along_frame(tile))
        finish(third_on(tile))
        return carry

    lax.fori_loop(0, 9, from_sibling, 0)
    finish(along_height())
    for hslot in range(3):
        finish(along_width(hslot))


def gather(keys, values):
    return pl.pallas_call(
        gather_kernel,
        out_shape=jax.ShapeDtypeStruct((27, 2, ROWS, DIM), jnp.bfloat16),
        in_specs=[pl.BlockSpec(memory_space=pltpu.VMEM)] * 2,
        out_specs=pl.BlockSpec(memory_space=pltpu.VMEM),
        scratch_shapes=[
            pltpu.SemaphoreType.DMA((3,)),
            pltpu.SemaphoreType.DMA((3, 3)),
            pltpu.SemaphoreType.DMA((9,)),
            pltpu.SemaphoreType.DMA((9,)),
            pltpu.SemaphoreType.DMA((9,)),
            pltpu.SemaphoreType.DMA((27,)),
        ],
        compiler_params=pltpu.CompilerParams(
            collective_id=0, has_side_effects=True, vmem_limit_bytes=LIMIT
        ),
        name="gather",
    )(keys, values)


def combine_kernel(
    parts,
    weight,
    kv_out,
    weight_out,
    half,
    pieces,
    lines,
    full,
    swap,
    third,
    cross,
    outgoing,
    wide,
    high,
    half_sem,
    piece_send,
    piece_recv,
    line_send,
    line_recv,
    full_send,
    pass_send,
    full_recv,
    swap_send,
    swap_recv,
    third_send,
    third_recv,
    cross_send,
    cross_recv,
    wide_send,
    wide_recv,
    high_send,
    high_recv,
):
    place = Place()
    greet_all(place)
    core, ring, h = place.core, place.ring, place.h
    own, sib, far = place.own_plane * 9, place.sib_plane * 9, place.third_plane * 9
    f32 = jnp.float32

    half_copy = remote(
        weight.at[1 - core], half, half_sem.at[0], half_sem.at[1], place.sibling
    )
    half_copy.start()

    def swap_copy(tile):
        return remote(
            parts.at[sib + tile], swap.at[tile], swap_send.at[tile], swap_recv.at[tile],
            place.sibling,
        )

    def third_copy(tile):
        return remote(
            parts.at[far + tile], third.at[tile], third_send.at[tile], third_recv.at[tile],
            place.sibling,
        )

    def cross_copy(tile):
        return remote(
            third.at[tile], cross.at[tile], cross_send.at[tile], cross_recv.at[tile],
            place.partner,
        )

    def start_third(tile, carry):
        third_copy(tile).start()
        return carry

    def start_swap(tile, carry):
        swap_copy(tile).start()
        return carry

    @pl.when(place.supplies)
    def _():
        lax.fori_loop(0, 9, start_third, 0)

    lax.fori_loop(0, 9, start_swap, 0)

    half_copy.wait()

    def add_half(piece, carry):
        rows = pl.ds(pl.multiple_of(piece * 96, 96), 96)
        half[rows] = (weight[core, rows].astype(f32) + half[rows].astype(f32)).astype(
            jnp.bfloat16
        )
        return carry

    lax.fori_loop(0, 16, add_half, 0)

    def piece_copy(k):
        to = lax.rem(ring + k, 16)
        rows = pl.ds(pl.multiple_of(to * 96, 96), 96)
        return remote(
            half.at[rows], pieces.at[ring], piece_send.at[to], piece_recv.at[ring],
            place.plane_chip(to),
        )

    def start_piece(k, carry):
        piece_copy(k).start()
        return carry

    lax.fori_loop(1, 16, start_piece, 0)

    @pl.when(place.collects)
    def _():
        def one(tile, carry):
            arrived(third.at[tile], third_recv.at[tile])
            third[tile] = (parts[far + tile].astype(f32) + third[tile].astype(f32)).astype(
                jnp.bfloat16
            )
            cross_copy(tile).start()
            return carry

        lax.fori_loop(0, 9, one, 0)

    mine = pl.ds(pl.multiple_of(ring * 96, 96), 96)

    def add_piece(k, total):
        other = lax.rem(ring + k, 16)
        arrived(pieces.at[other], piece_recv.at[other])
        return total + pieces[other].astype(f32)

    total = lax.fori_loop(1, 16, add_piece, half[mine].astype(f32))
    lines[h] = total.astype(jnp.bfloat16)

    def line_copy(k):
        to = lax.rem(h + k, 8)
        return remote(
            lines.at[h], lines.at[h], line_send.at[to], line_recv.at[h],
            (place.f, to, place.w),
        )

    def start_line(k, carry):
        line_copy(k).start()
        return carry

    lax.fori_loop(1, 8, start_line, 0)

    def own_tile(tile):
        arrived(swap.at[tile], swap_recv.at[tile])
        outgoing[tile] = parts[own + tile].astype(f32) + swap[tile].astype(f32)

        @pl.when(place.supplies)
        def _():
            arrived(cross.at[tile], cross_recv.at[tile])
            outgoing[tile] += cross[tile].astype(f32)

        swap[tile] = outgoing[tile].astype(jnp.bfloat16)

    def width_copy(i, w, hslot):
        tile = (w - start(place.w)) * 3 + hslot
        back = (1, 0, 2)[i]
        return remote(
            swap.at[tile], wide.at[back, hslot], wide_send.at[i, hslot],
            wide_recv.at[back, hslot], (place.f, h, w),
        )

    for i, (there, w) in enumerate(owners(place.w)):

        @pl.when(there)
        def _():
            def one(hslot, carry):
                own_tile((w - start(place.w)) * 3 + hslot)
                width_copy(i, w, hslot).start()
                return carry

            lax.fori_loop(0, 3, one, 0)

    def add_line(k, total):
        other = lax.rem(h + k, 8)
        arrived(lines.at[other], line_recv.at[other])
        return total + lines[other].astype(f32)

    total = lax.fori_loop(1, 8, add_line, total)
    full[core, mine] = (total * (1.0 / 256.0)).astype(jnp.bfloat16)

    def full_copy(k):
        to = lax.rem(ring + k, 16)
        return remote(
            full.at[core, mine], full.at[core, mine], full_send.at[to], full_recv.at[core, ring],
            place.plane_chip(to),
        )

    def pass_copy(piece):
        rows = pl.ds(pl.multiple_of(piece * 96, 96), 96)
        return remote(
            full.at[core, rows], full.at[core, rows], pass_send.at[piece],
            full_recv.at[core, piece], place.sibling,
        )

    def start_full(k, carry):
        full_copy(k).start()
        return carry

    lax.fori_loop(1, 16, start_full, 0)
    pass_copy(ring).start()

    def own_column(hslot, carry):
        own_tile(place.wslot * 3 + hslot)
        return carry

    lax.fori_loop(0, 3, own_column, 0)
    for i, (there, _w) in enumerate(neighbours(place.w)):

        @pl.when(there)
        def _():
            def one(hslot, carry):
                arrived(wide.at[i, hslot], wide_recv.at[i, hslot])
                outgoing[place.wslot * 3 + hslot] += wide[i, hslot].astype(f32)
                return carry

            lax.fori_loop(0, 3, one, 0)

    def height_copy(i, to):
        hslot = to - start(h)
        back = (1, 0, 2)[i]
        return remote(
            swap.at[place.wslot * 3 + hslot], high.at[back], high_send.at[i],
            high_recv.at[back], (place.f, to, place.w),
        )

    for i, (there, to) in enumerate(owners(h)):

        @pl.when(there)
        def _():
            tile = place.wslot * 3 + to - start(h)
            swap[tile] = outgoing[tile].astype(jnp.bfloat16)
            height_copy(i, to).start()

    def pass_on(k, carry):
        other = lax.rem(ring + k, 16)
        rows = pl.ds(pl.multiple_of(other * 96, 96), 96)
        arrived(full.at[core, rows], full_recv.at[core, other])
        pass_copy(other).start()
        return carry

    lax.fori_loop(1, 16, pass_on, 0)

    tile = place.wslot * 3 + place.hslot
    for i, (there, _h) in enumerate(neighbours(h)):

        @pl.when(there)
        def _():
            arrived(high.at[i], high_recv.at[i])
            outgoing[tile] += high[i].astype(f32)

    kv_out[...] = outgoing[tile].astype(jnp.bfloat16)

    def take_rest(piece, carry):
        rows = pl.ds(pl.multiple_of(piece * 96, 96), 96)
        arrived(full.at[1 - core, rows], full_recv.at[1 - core, piece])
        return carry

    lax.fori_loop(0, 16, take_rest, 0)
    for side in range(2):
        for block in range(12):
            weight_out[:, (side * 12 + block) * 128 : (side * 12 + block + 1) * 128] = full[
                side, block * 128 : (block + 1) * 128
            ].astype(f32)

    def left_plane(k, carry):
        piece_copy(k).wait_send()
        full_copy(k).wait_send()
        return carry

    lax.fori_loop(1, 16, left_plane, 0)

    def left_line(k, carry):
        line_copy(k).wait_send()
        return carry

    lax.fori_loop(1, 8, left_line, 0)

    def left_pass(piece, carry):
        pass_copy(piece).wait_send()
        return carry

    lax.fori_loop(0, 16, left_pass, 0)

    def left_tile(tile, carry):
        swap_copy(tile).wait_send()
        pl.when(place.supplies)(third_copy(tile).wait_send)
        pl.when(place.collects)(cross_copy(tile).wait_send)
        return carry

    lax.fori_loop(0, 9, left_tile, 0)
    for i, (there, w) in enumerate(owners(place.w)):
        for hslot in range(3):
            pl.when(there)(width_copy(i, w, hslot).wait_send)
    for i, (there, to) in enumerate(owners(h)):
        pl.when(there)(height_copy(i, to).wait_send)


def combine(parts, weight):
    bf16, f32 = jnp.bfloat16, jnp.float32
    vmem, dma = pltpu.VMEM, pltpu.SemaphoreType.DMA
    return pl.pallas_call(
        combine_kernel,
        out_shape=(
            jax.ShapeDtypeStruct((2, ROWS, DIM), bf16),
            jax.ShapeDtypeStruct((DIM, 3072), f32),
        ),
        in_specs=[pl.BlockSpec(memory_space=pltpu.VMEM)] * 2,
        out_specs=[pl.BlockSpec(memory_space=pltpu.VMEM)] * 2,
        scratch_shapes=[
            vmem((1536, DIM), bf16),
            vmem((16, 96, DIM), bf16),
            vmem((8, 96, DIM), bf16),
            vmem((2, 1536, DIM), bf16),
            vmem((9, 2, ROWS, DIM), bf16),
            vmem((9, 2, ROWS, DIM), bf16),
            vmem((9, 2, ROWS, DIM), bf16),
            vmem((9, 2, ROWS, DIM), f32),
            vmem((3, 3, 2, ROWS, DIM), bf16),
            vmem((3, 2, ROWS, DIM), bf16),
            dma((2,)),
            dma((16,)),
            dma((16,)),
            dma((8,)),
            dma((8,)),
            dma((16,)),
            dma((16,)),
            dma((2, 16)),
            dma((9,)),
            dma((9,)),
            dma((9,)),
            dma((9,)),
            dma((9,)),
            dma((9,)),
            dma((3, 3)),
            dma((3, 3)),
            dma((3,)),
            dma((3,)),
        ],
        compiler_params=pltpu.CompilerParams(
            collective_id=1, has_side_effects=True, vmem_limit_bytes=LIMIT
        ),
        name="combine",
    )(parts, weight)


def body(queries, key_vectors, value_vectors, out_weight, projected_grad):
    f32, bf16 = jnp.float32, jnp.bfloat16
    model_dim = out_weight.shape[1]
    inv_root = 1.0 / math.sqrt(DIM)
    dot = functools.partial(jnp.einsum, preferred_element_type=f32)
    window = gather(key_vectors.reshape(ROWS, DIM), value_vectors.reshape(ROWS, DIM))
    key_rows = window[:, 0].reshape(-1, DIM)
    value_rows = window[:, 1].reshape(-1, DIM)
    query_rows = queries.reshape(-1, DIM)
    grad_rows = projected_grad.reshape(-1, model_dim)
    scores = dot("qd,kd->qk", query_rows, key_rows) * inv_root
    row_max = jnp.max(scores, axis=1, keepdims=True)
    weights = jnp.exp(scores - row_max)
    probability = weights / jnp.sum(weights, axis=1, keepdims=True)
    prob_bf = probability.astype(bf16)
    attended = dot("qk,kd->qd", prob_bf, value_rows).astype(bf16)
    projected = dot("qd,dm->qm", attended, out_weight).astype(bf16)
    attended_grad = dot("tm,dm->td", grad_rows, out_weight).astype(bf16)
    weight_term = dot("td,tm->dm", attended, grad_rows).astype(bf16)
    row_dot = jnp.sum(attended_grad.astype(f32) * attended.astype(f32), axis=1, keepdims=True)
    prob_grad = dot("qd,kd->qk", attended_grad, value_rows)
    score_grad = (probability * (prob_grad - row_dot)).astype(bf16)
    grad_query = (dot("qk,kd->qd", score_grad, key_rows) * inv_root).astype(bf16)
    key_part = (dot("qk,qd->kd", score_grad, query_rows) * inv_root).astype(bf16)
    value_part = dot("qk,qd->kd", prob_bf, attended_grad).astype(bf16)
    parts = jnp.stack(
        (key_part.reshape(27, ROWS, DIM), value_part.reshape(27, ROWS, DIM)), axis=1
    )
    halves = weight_term.reshape(DIM, 2, 12, 128).transpose(1, 2, 0, 3).reshape(2, 1536, 128)
    kv_grad, grad_out_weight = combine(parts, halves)
    return (
        projected.reshape(projected_grad.shape),
        grad_query.reshape(queries.shape),
        kv_grad[0].reshape(queries.shape),
        kv_grad[1].reshape(queries.shape),
        grad_out_weight,
    )


def solution(mesh):
    spec = P("frame", "height", "width", None)
    return jax.shard_map(
        body,
        mesh=mesh,
        in_specs=(spec, spec, spec, P(), spec),
        out_specs=(spec, spec, spec, spec, P()),
        check_vma=False,
    )
```

```python
import math

import jax
import jax.experimental.pallas as pl
import jax.experimental.pallas.tpu as pltpu
import jax.numpy as jnp
from jax import lax
from jax.sharding import PartitionSpec as P

MESH = pl.DeviceIdType.MESH
ROWS = 192
DIM = 128
LIMIT = 56 * 2**20
BF16, F32 = jnp.bfloat16, jnp.float32
ROOT = 1.0 / math.sqrt(DIM)
SCALE = ROOT * math.log2(math.e)


class Place:
    def __init__(self):
        self.f = lax.axis_index("frame")
        self.h = lax.axis_index("height")
        self.w = lax.axis_index("width")
        self.xlo = self.f // 2
        self.core = self.f - 2 * self.xlo
        self.xhi = self.w // 4
        self.y = self.w - 4 * self.xhi
        self.ring = (2 * self.xhi + self.xlo) * 4 + self.y
        self.sibling = (self.xlo * 2 + 1 - self.core, self.h, self.w)
        self.partner = ((1 - self.xlo) * 2 + self.core, self.h, self.w)
        self.own_plane = self.f - self.xlo
        self.sib_plane = self.xlo * 2 + 1 - self.core - self.xlo
        self.third_plane = 2 * (1 - self.xlo)
        self.collects = self.core == self.xlo
        self.supplies = self.core != self.xlo
        self.hslot = self.h - start(self.h)
        self.wslot = self.w - start(self.w)

    def plane_chip(self, index):
        x = index // 4
        y = index - 4 * x
        xhi = x // 2
        return ((x - 2 * xhi) * 2 + self.core, self.h, xhi * 4 + y)


def start(index):
    return jnp.maximum(jnp.minimum(index - 1, 5), 0)


def neighbours(index):
    return (
        (index >= 1, index - 1),
        (index <= 6, index + 1),
        ((index == 2) | (index == 5), 7 * (index // 5)),
    )


def owners(index):
    return (
        (index >= 1, index - 1),
        (index <= 6, index + 1),
        ((index == 0) | (index == 7), 2 + 3 * (index // 7)),
    )


def remote(src, dst, send_sem, recv_sem, target):
    return pltpu.make_async_remote_copy(
        src_ref=src,
        dst_ref=dst,
        send_sem=send_sem,
        recv_sem=recv_sem,
        device_id=target,
        device_id_type=MESH,
    )


def arrived(ref, sem):
    pltpu.make_async_copy(ref, ref, sem).wait()


def greet_plane(place, barrier):
    def one(k, carry):
        target = place.plane_chip(lax.rem(place.ring + k, 16))
        pl.semaphore_signal(barrier, inc=1, device_id=target, device_id_type=MESH)
        return carry

    lax.fori_loop(1, 16, one, 0)


def greet_column(place, barrier):
    def one(k, carry):
        target = (place.f, lax.rem(place.h + k, 8), place.w)
        pl.semaphore_signal(barrier, inc=1, device_id=target, device_id_type=MESH)
        return carry

    lax.fori_loop(1, 8, one, 0)


def greet_all(place):
    barrier = pltpu.get_barrier_semaphore()
    pl.semaphore_signal(barrier, inc=1, device_id=place.sibling, device_id_type=MESH)
    greet_plane(place, barrier)
    greet_column(place, barrier)
    pl.semaphore_wait(barrier, 23)


def begin(copies):
    for there, copy in copies:
        if there is True:
            copy.start()
        else:
            pl.when(there)(copy.start)


def finish(copies):
    for there, copy in copies:
        if there is True:
            copy.wait_send()
        else:
            pl.when(there)(copy.wait_send)


def tile_of(hslot):
    return pl.ds(pl.multiple_of(hslot * ROWS, ROWS), ROWS)


def piece_of(index):
    return pl.ds(pl.multiple_of(index * 96, 96), 96)


def dot(left, right, over):
    return lax.dot_general(left, right, ((over[:1], over[1:]), ((), ())), preferred_element_type=F32)


def kernel(
    q_ref, k_ref, v_ref, weight_hbm, grad_hbm,
    projected_hbm, query_out, kv_out, weight_out,
    kv, prob, prob_grad, col_max, run_max, run_sum, att, dquery, dout, dots,
    grads, weight, projected,
    terms, half, pieces, lines, full,
    parts, swap, third, cross, outgoing, wide, high,
    load_sem, store_sem,
    hsend, wsend, ssend, tsend, xsend, recv,
    half_sem, piece_send, piece_recv, line_send, line_recv, full_send, pass_send, full_recv,
    swap_send, swap_recv, third_send, third_recv, cross_send, cross_recv,
    wide_send, wide_recv, high_send, high_recv,
):
    place = Place()
    core, ring, h = place.core, place.ring, place.h
    own, sib, far = place.own_plane * 3, place.sib_plane * 3, place.third_plane * 3
    hslots = (place.hslot, lax.rem(place.hslot + 1, 3), lax.rem(place.hslot + 2, 3))
    wslots = (place.wslot, lax.rem(place.wslot + 1, 3), lax.rem(place.wslot + 2, 3))

    load_grads = pltpu.make_async_copy(grad_hbm, grads, load_sem.at[0])
    load_weight = pltpu.make_async_copy(weight_hbm, weight, load_sem.at[1])
    load_grads.start()
    load_weight.start()
    kv[own + place.wslot, 0, tile_of(place.hslot)] = k_ref[...]
    kv[own + place.wslot, 1, tile_of(place.hslot)] = v_ref[...]
    run_max[...] = jnp.full(run_max.shape, -jnp.inf, F32)
    run_sum[...] = jnp.zeros(run_sum.shape, F32)
    att[...] = jnp.zeros(att.shape, F32)
    dquery[...] = jnp.zeros(dquery.shape, F32)
    greet_all(place)

    def window(col, hslot):
        return kv.at[col, :, tile_of(hslot)]

    def along_height():
        col = own + place.wslot
        for i, (there, to) in enumerate(neighbours(h)):
            slot = h - start(to)
            yield there, remote(
                window(col, place.hslot), window(col, slot), hsend.at[i], recv.at[col, slot],
                (place.f, to, place.w),
            )

    def along_width(hslot):
        for i, (there, to) in enumerate(neighbours(place.w)):
            col = own + place.w - start(to)
            yield there, remote(
                window(own + place.wslot, hslot), window(col, hslot), wsend.at[i, hslot],
                recv.at[col, hslot], (place.f, h, to),
            )

    def along_frame(wslot, hslot):
        col = own + wslot
        to = 6 * place.xlo + wslot
        yield True, remote(
            window(col, hslot), window(col, hslot), ssend.at[wslot, hslot], recv.at[col, hslot],
            place.sibling,
        )
        yield place.supplies, remote(
            window(col, hslot), window(to, hslot), xsend.at[wslot, hslot], recv.at[to, hslot],
            place.partner,
        )

    def third_on(wslot, hslot):
        col = far + wslot
        yield place.collects, remote(
            window(col, hslot), window(col, hslot), tsend.at[wslot, hslot], recv.at[col, hslot],
            place.sibling,
        )

    def take(col, hslot):
        arrived(window(col, hslot), recv.at[col, hslot])

    def forward(col):
        keys, values = kv[col, 0], kv[col, 1]
        scores = dot(keys, q_ref[...], (1, 1))
        before = run_max[...]
        now = jnp.maximum(before, jnp.max(scores, axis=0, keepdims=True))
        shrink = jnp.exp2((before - now) * SCALE)
        weights = jnp.exp2((scores - now) * SCALE)
        run_max[...] = now
        col_max[col] = now
        run_sum[...] = run_sum[...] * shrink + jnp.sum(weights, axis=0, keepdims=True)
        prob[col] = weights
        att[...] = att[...] * shrink + dot(values, weights.astype(BF16), (0, 0))
        prob_grad[col] = dot(values, dout[...], (1, 1))

    begin(along_height())
    begin(along_width(hslots[0]))
    begin(along_frame(wslots[0], hslots[0]))
    load_grads.wait()
    load_weight.wait()
    dout[...] = dot(grads[...], weight[...], (1, 1)).astype(BF16)
    for hslot in hslots[1:]:
        take(own + wslots[0], hslot)
        begin(along_width(hslot))
        begin(along_frame(wslots[0], hslot))
    forward(own + wslots[0])
    for hslot in hslots[:2]:
        for wslot in wslots[1:]:
            take(own + wslot, hslot)
            begin(along_frame(wslot, hslot))
    for hslot in hslots:
        take(sib + wslots[0], hslot)
    forward(sib + wslots[0])
    for wslot in wslots[1:]:
        take(own + wslot, hslots[2])
        begin(along_frame(wslot, hslots[2]))
    for hslot in hslots:
        take(far + wslots[0], hslot)
        begin(third_on(wslots[0], hslot))
    forward(own + wslots[1])
    forward(far + wslots[0])
    for hslot in hslots[:2]:
        for wslot in wslots[1:]:
            take(far + wslot, hslot)
            begin(third_on(wslot, hslot))
    forward(own + wslots[2])
    for wslot in wslots[1:]:
        take(far + wslot, hslots[2])
        begin(third_on(wslot, hslots[2]))
    for wslot in wslots[1:]:
        for hslot in hslots:
            take(sib + wslot, hslot)
        forward(sib + wslot)
    for wslot in wslots[1:]:
        forward(far + wslot)

    inverse = 1.0 / run_sum[...]
    attended = (att[...] * inverse).astype(BF16)

    def weight_terms(side):
        def one(i, carry):
            columns = pl.ds(pl.multiple_of(side * 1536 + i * 512, 512), 512)
            term = dot(attended, grads[:, columns], (1, 0)).astype(BF16)
            for j in range(4):
                rows = pl.ds(pl.multiple_of(i * 512 + j * 128, 128), 128)
                terms[side, rows] = term[:, j * 128 : (j + 1) * 128]
            return carry

        lax.fori_loop(0, 3, one, 0)

    half_copy = remote(terms.at[1 - core], half, half_sem.at[0], half_sem.at[1], place.sibling)
    weight_terms(1 - core)
    half_copy.start()
    weight_terms(core)
    dots[...] = jnp.sum(
        jnp.transpose(dout[...].astype(F32)) * attended.astype(F32), axis=0, keepdims=True
    )

    def backward(col):
        share = jnp.exp2((col_max[col] - run_max[...]) * SCALE) / run_sum[...]
        probability = prob[col] * share
        score_grad = (probability * (prob_grad[col] - dots[...])).astype(BF16)
        parts[col, 1] = dot(probability.astype(BF16), dout[...], (1, 0)).astype(BF16)
        parts[col, 0] = (dot(score_grad, q_ref[...], (1, 0)) * ROOT).astype(BF16)
        dquery[...] += dot(kv[col, 0], score_grad, (0, 0))

    def swap_copy(wslot):
        return remote(
            parts.at[sib + wslot], swap.at[wslot], swap_send.at[wslot], swap_recv.at[wslot],
            place.sibling,
        )

    def third_copy(wslot):
        return remote(
            parts.at[far + wslot], third.at[wslot], third_send.at[wslot], third_recv.at[wslot],
            place.sibling,
        )

    def cross_copy(wslot, hslot):
        rows = tile_of(hslot)
        return remote(
            third.at[wslot, :, rows], cross.at[wslot, :, rows], cross_send.at[wslot, hslot],
            cross_recv.at[wslot, hslot], place.partner,
        )

    def third_column(wslot, carry):
        backward(far + wslot)
        pl.when(place.supplies)(third_copy(wslot).start)
        return carry

    lax.fori_loop(0, 3, third_column, 0)

    half_copy.wait()

    def add_half(piece, carry):
        rows = piece_of(piece)
        half[rows] = (terms[core, rows].astype(F32) + half[rows].astype(F32)).astype(BF16)
        return carry

    lax.fori_loop(0, 16, add_half, 0)

    def piece_copy(k):
        to = lax.rem(ring + k, 16)
        return remote(
            half.at[piece_of(to)], pieces.at[ring], piece_send.at[to], piece_recv.at[ring],
            place.plane_chip(to),
        )

    def start_piece(k, carry):
        piece_copy(k).start()
        return carry

    lax.fori_loop(1, 16, start_piece, 0)

    def sibling_column(wslot, carry):
        backward(sib + wslot)
        swap_copy(wslot).start()
        return carry

    lax.fori_loop(0, 3, sibling_column, 0)

    @pl.when(place.collects)
    def _():
        def one(wslot, carry):
            arrived(third.at[wslot], third_recv.at[wslot])
            for hslot in range(3):
                rows = tile_of(hslot)
                third[wslot, :, rows] = (
                    parts[far + wslot, :, rows].astype(F32) + third[wslot, :, rows].astype(F32)
                ).astype(BF16)
                cross_copy(wslot, hslot).start()
            return carry

        lax.fori_loop(0, 3, one, 0)

    def own_column(wslot, carry):
        backward(own + wslot)
        return carry

    lax.fori_loop(0, 3, own_column, 0)
    query_out[...] = (jnp.transpose(dquery[...]) * ROOT).astype(BF16)

    def project(i, carry):
        columns = pl.ds(pl.multiple_of(i * 512, 512), 512)
        projected[:, columns] = dot(attended, weight[:, columns], (0, 0)).astype(BF16)
        return carry

    lax.fori_loop(0, 6, project, 0)
    store = pltpu.make_async_copy(projected, projected_hbm, store_sem)
    store.start()

    mine = piece_of(ring)

    def add_piece(k, total):
        other = lax.rem(ring + k, 16)
        arrived(pieces.at[other], piece_recv.at[other])
        return total + pieces[other].astype(F32)

    total = lax.fori_loop(1, 16, add_piece, half[mine].astype(F32))
    lines[h] = total.astype(BF16)

    def line_copy(k):
        to = lax.rem(h + k, 8)
        return remote(
            lines.at[h], lines.at[h], line_send.at[to], line_recv.at[h], (place.f, to, place.w)
        )

    def start_line(k, carry):
        line_copy(k).start()
        return carry

    lax.fori_loop(1, 8, start_line, 0)

    def own_tile(wslot, hslot):
        rows = tile_of(hslot)
        outgoing[wslot, :, rows] = parts[own + wslot, :, rows].astype(F32) + swap[
            wslot, :, rows
        ].astype(F32)

        @pl.when(place.supplies)
        def _():
            arrived(cross.at[wslot, :, rows], cross_recv.at[wslot, hslot])
            outgoing[wslot, :, rows] += cross[wslot, :, rows].astype(F32)

        swap[wslot, :, rows] = outgoing[wslot, :, rows].astype(BF16)

    def width_copy(i, to, hslot):
        back = (1, 0, 2)[i]
        return remote(
            swap.at[to - start(place.w), :, tile_of(hslot)], wide.at[back, hslot],
            wide_send.at[i, hslot], wide_recv.at[back, hslot], (place.f, h, to),
        )

    for i, (there, to) in enumerate(owners(place.w)):

        @pl.when(there)
        def _():
            wslot = to - start(place.w)
            arrived(swap.at[wslot], swap_recv.at[wslot])

            def one(hslot, carry):
                own_tile(wslot, hslot)
                width_copy(i, to, hslot).start()
                return carry

            lax.fori_loop(0, 3, one, 0)

    def add_line(k, total):
        other = lax.rem(h + k, 8)
        arrived(lines.at[other], line_recv.at[other])
        return total + lines[other].astype(F32)

    total = lax.fori_loop(1, 8, add_line, total)
    full[core, mine] = (total * (1.0 / 256.0)).astype(BF16)

    def full_copy(k):
        to = lax.rem(ring + k, 16)
        return remote(
            full.at[core, mine], full.at[core, mine], full_send.at[to], full_recv.at[core, ring],
            place.plane_chip(to),
        )

    def pass_copy(piece):
        rows = piece_of(piece)
        return remote(
            full.at[core, rows], full.at[core, rows], pass_send.at[piece],
            full_recv.at[core, piece], place.sibling,
        )

    def start_full(k, carry):
        full_copy(k).start()
        return carry

    lax.fori_loop(1, 16, start_full, 0)
    pass_copy(ring).start()

    arrived(swap.at[place.wslot], swap_recv.at[place.wslot])

    def own_rows(hslot, carry):
        own_tile(place.wslot, hslot)
        return carry

    lax.fori_loop(0, 3, own_rows, 0)
    for i, (there, _w) in enumerate(neighbours(place.w)):

        @pl.when(there)
        def _():
            def one(hslot, carry):
                arrived(wide.at[i, hslot], wide_recv.at[i, hslot])
                outgoing[place.wslot, :, tile_of(hslot)] += wide[i, hslot].astype(F32)
                return carry

            lax.fori_loop(0, 3, one, 0)

    def height_copy(i, to):
        rows = tile_of(to - start(h))
        back = (1, 0, 2)[i]
        return remote(
            swap.at[place.wslot, :, rows], high.at[back], high_send.at[i], high_recv.at[back],
            (place.f, to, place.w),
        )

    for i, (there, to) in enumerate(owners(h)):

        @pl.when(there)
        def _():
            rows = tile_of(to - start(h))
            swap[place.wslot, :, rows] = outgoing[place.wslot, :, rows].astype(BF16)
            height_copy(i, to).start()

    def pass_on(k, carry):
        other = lax.rem(ring + k, 16)
        arrived(full.at[core, piece_of(other)], full_recv.at[core, other])
        pass_copy(other).start()
        return carry

    lax.fori_loop(1, 16, pass_on, 0)
    rows = tile_of(place.hslot)
    for i, (there, _h) in enumerate(neighbours(h)):

        @pl.when(there)
        def _():
            arrived(high.at[i], high_recv.at[i])
            outgoing[place.wslot, :, rows] += high[i].astype(F32)

    kv_out[...] = outgoing[place.wslot, :, rows].astype(BF16)

    def take_rest(piece, carry):
        arrived(full.at[1 - core, piece_of(piece)], full_recv.at[1 - core, piece])
        return carry

    lax.fori_loop(0, 16, take_rest, 0)
    for side in range(2):
        for block in range(12):
            weight_out[:, (side * 12 + block) * 128 : (side * 12 + block + 1) * 128] = full[
                side, block * 128 : (block + 1) * 128
            ].astype(F32)

    def left_plane(k, carry):
        piece_copy(k).wait_send()
        full_copy(k).wait_send()
        return carry

    lax.fori_loop(1, 16, left_plane, 0)

    def left_line(k, carry):
        line_copy(k).wait_send()
        return carry

    lax.fori_loop(1, 8, left_line, 0)

    def left_pass(piece, carry):
        pass_copy(piece).wait_send()
        return carry

    lax.fori_loop(0, 16, left_pass, 0)
    finish(along_height())

    def left_column(wslot, carry):
        swap_copy(wslot).wait_send()
        pl.when(place.supplies)(third_copy(wslot).wait_send)
        for hslot in range(3):
            finish(along_frame(wslot, hslot))
            finish(third_on(wslot, hslot))
            pl.when(place.collects)(cross_copy(wslot, hslot).wait_send)
        return carry

    lax.fori_loop(0, 3, left_column, 0)
    for hslot in range(3):
        finish(along_width(hslot))
    for i, (there, to) in enumerate(owners(place.w)):
        for hslot in range(3):
            pl.when(there)(width_copy(i, to, hslot).wait_send)
    for i, (there, to) in enumerate(owners(h)):
        pl.when(there)(height_copy(i, to).wait_send)
    store.wait()


def body(queries, key_vectors, value_vectors, out_weight, projected_grad):
    vmem, dma = pltpu.VMEM, pltpu.SemaphoreType.DMA
    model = out_weight.shape[1]
    column = (2, 3 * ROWS, DIM)
    here, there = pl.BlockSpec(memory_space=pltpu.VMEM), pl.BlockSpec(memory_space=pl.ANY)
    tile = (ROWS, DIM)
    projected, grad_query, kv_grad, grad_out_weight = pl.pallas_call(
        kernel,
        out_shape=(
            jax.ShapeDtypeStruct((ROWS, model), BF16),
            jax.ShapeDtypeStruct(tile, BF16),
            jax.ShapeDtypeStruct((2, ROWS, DIM), BF16),
            jax.ShapeDtypeStruct((DIM, model), F32),
        ),
        in_specs=[here, here, here, there, there],
        out_specs=[there, here, here, here],
        scratch_shapes=[
            vmem((9,) + column, BF16),
            vmem((9, 3 * ROWS, ROWS), F32),
            vmem((9, 3 * ROWS, ROWS), F32),
            vmem((9, 1, ROWS), F32),
            vmem((1, ROWS), F32),
            vmem((1, ROWS), F32),
            vmem((DIM, ROWS), F32),
            vmem((DIM, ROWS), F32),
            vmem(tile, BF16),
            vmem((1, ROWS), F32),
            vmem((ROWS, model), BF16),
            vmem((DIM, model), BF16),
            vmem((ROWS, model), BF16),
            vmem((2, 1536, DIM), BF16),
            vmem((1536, DIM), BF16),
            vmem((16, 96, DIM), BF16),
            vmem((8, 96, DIM), BF16),
            vmem((2, 1536, DIM), BF16),
            vmem((9,) + column, BF16),
            vmem((3,) + column, BF16),
            vmem((3,) + column, BF16),
            vmem((3,) + column, BF16),
            vmem((3,) + column, F32),
            vmem((3, 3, 2, ROWS, DIM), BF16),
            vmem((3, 2, ROWS, DIM), BF16),
            dma((2,)),
            dma,
            dma((3,)),
            dma((3, 3)),
            dma((3, 3)),
            dma((3, 3)),
            dma((3, 3)),
            dma((9, 3)),
            dma((2,)),
            dma((16,)),
            dma((16,)),
            dma((8,)),
            dma((8,)),
            dma((16,)),
            dma((16,)),
            dma((2, 16)),
            dma((3,)),
            dma((3,)),
            dma((3,)),
            dma((3,)),
            dma((3, 3)),
            dma((3, 3)),
            dma((3, 3)),
            dma((3, 3)),
            dma((3,)),
            dma((3,)),
        ],
        compiler_params=pltpu.CompilerParams(
            collective_id=0, has_side_effects=True, vmem_limit_bytes=LIMIT
        ),
        name="attention",
    )(
        queries.reshape(tile),
        key_vectors.reshape(tile),
        value_vectors.reshape(tile),
        out_weight,
        projected_grad.reshape(ROWS, model),
    )
    return (
        projected.reshape(projected_grad.shape),
        grad_query.reshape(queries.shape),
        kv_grad[0].reshape(queries.shape),
        kv_grad[1].reshape(queries.shape),
        grad_out_weight,
    )


def solution(mesh):
    spec = P("frame", "height", "width", None)
    return jax.shard_map(
        body,
        mesh=mesh,
        in_specs=(spec, spec, spec, P(), spec),
        out_specs=(spec, spec, spec, spec, P()),
        check_vma=False,
    )
```

```python
import math

import jax
import jax.experimental.pallas as pl
import jax.experimental.pallas.tpu as pltpu
import jax.numpy as jnp
from jax import lax
from jax.sharding import PartitionSpec as P

MESH = pl.DeviceIdType.MESH
ROWS = 192
WIDE = 256
DIM = 128
LIMIT = 56 * 2**20
BF16, F32 = jnp.bfloat16, jnp.float32
ROOT = 1.0 / math.sqrt(DIM)
SCALE = ROOT * math.log2(math.e)


class Place:
    def __init__(self):
        self.f = lax.axis_index("frame")
        self.h = lax.axis_index("height")
        self.w = lax.axis_index("width")
        self.xlo = self.f // 2
        self.core = self.f - 2 * self.xlo
        self.xhi = self.w // 4
        self.y = self.w - 4 * self.xhi
        self.ring = (2 * self.xhi + self.xlo) * 4 + self.y
        self.sibling = (self.xlo * 2 + 1 - self.core, self.h, self.w)
        self.partner = ((1 - self.xlo) * 2 + self.core, self.h, self.w)
        self.own_plane = self.core
        self.sib_plane = 1 - self.core
        self.lent_plane = 1 - self.xlo
        self.lends_own = self.core != self.xlo
        self.lends_sib = self.core == self.xlo
        self.hslot = self.h - start(self.h)
        self.wslot = self.w - start(self.w)

    def plane_chip(self, index):
        x = index // 4
        y = index - 4 * x
        xhi = x // 2
        return ((x - 2 * xhi) * 2 + self.core, self.h, xhi * 4 + y)

    def plane_shift(self, k):
        x = lax.rem(2 * self.xhi + self.xlo + k // 4, 4)
        return x * 4 + lax.rem(self.y + lax.rem(k, 4), 4)


def start(index):
    return jnp.maximum(jnp.minimum(index - 1, 5), 0)


def neighbours(index):
    return (
        (index >= 1, index - 1),
        (index <= 6, index + 1),
        ((index == 2) | (index == 5), 7 * (index // 5)),
    )


def owners(index):
    return (
        (index >= 1, index - 1),
        (index <= 6, index + 1),
        ((index == 0) | (index == 7), 2 + 3 * (index // 7)),
    )


def remote(src, dst, send_sem, recv_sem, target):
    return pltpu.make_async_remote_copy(
        src_ref=src,
        dst_ref=dst,
        send_sem=send_sem,
        recv_sem=recv_sem,
        device_id=target,
        device_id_type=MESH,
    )


def arrived(ref, sem):
    pltpu.make_async_copy(ref, ref, sem).wait()


def greet_all(place):
    barrier = pltpu.get_barrier_semaphore()

    def greet(target):
        pl.semaphore_signal(barrier, inc=1, device_id=target, device_id_type=MESH)

    for k in (4, 3, 5, 2, 6):
        greet((place.f, lax.rem(place.h + k, 8), place.w))
    for k in (10, 6, 9, 11, 14, 2, 5, 7, 8, 13, 15, 1, 3, 4, 12):
        greet(place.plane_chip(place.plane_shift(k)))
    for k in (1, 7):
        greet((place.f, lax.rem(place.h + k, 8), place.w))
    greet(place.sibling)


def begin(copies):
    for there, copy in copies:
        if there is True:
            copy.start()
        else:
            pl.when(there)(copy.start)


def finish(copies):
    for there, copy in copies:
        if there is True:
            copy.wait_send()
        else:
            pl.when(there)(copy.wait_send)


def tile_of(hslot):
    return pl.ds(pl.multiple_of(hslot * ROWS, ROWS), ROWS)


def piece_of(index, chunk):
    return pl.ds(pl.multiple_of(index * 96 + chunk * 48, 48), 48)


def far_first(i):
    return 1 + lax.rem(i + 9, 15)


def dot(left, right, over):
    return lax.dot_general(left, right, ((over[:1], over[1:]), ((), ())), preferred_element_type=F32)


def kernel(
    q_ref, k_ref, v_ref, weight_hbm, grad_hbm,
    projected_hbm, query_out, kv_out, full,
    kv, queries, douts, own_prob, own_grad, own_max, lent_prob, lent_grad, lent_max,
    own_state, lent_state, own_att, lent_att, att_out, att_in, state_out, state_in,
    stats_out, stats_in, dquery, dquery_out, dquery_in,
    grads, weight, projected,
    terms, half, pieces, lines,
    parts, swap, outgoing, wide, tall, high, side,
    load_sem, store_sem,
    hsend, wsend, ssend, recv, xsend, xrecv,
    half_sem, piece_send, piece_recv, line_send, line_recv, full_send, pass_send, full_recv,
    swap_send, swap_recv, wide_send, wide_recv, tall_send, tall_recv,
    high_send, high_recv, side_send, side_recv,
):
    place = Place()
    core, ring, h = place.core, place.ring, place.h
    own, sib, lent = place.own_plane * 3, place.sib_plane * 3, place.lent_plane * 3
    kept = 3 - lent
    hslots = (place.hslot, lax.rem(place.hslot + 1, 3), lax.rem(place.hslot + 2, 3))
    wslots = (place.wslot, lax.rem(place.wslot + 1, 3), lax.rem(place.wslot + 2, 3))
    mine, theirs = pl.ds(0, ROWS), pl.ds(WIDE, ROWS)

    greet_all(place)
    load_grads = pltpu.make_async_copy(grad_hbm, grads, load_sem.at[0])
    load_weight = pltpu.make_async_copy(weight_hbm, weight, load_sem.at[1])
    load_grads.start()
    load_weight.start()
    kv[own + place.wslot, 0, tile_of(place.hslot)] = k_ref[...]
    kv[own + place.wslot, 1, tile_of(place.hslot)] = v_ref[...]
    queries[mine] = q_ref[...]
    for first in (ROWS, WIDE + ROWS):
        queries[first : first + WIDE - ROWS] = jnp.zeros((WIDE - ROWS, DIM), BF16)
        douts[first : first + WIDE - ROWS] = jnp.zeros((WIDE - ROWS, DIM), BF16)
    for state, total in ((own_state, own_att), (lent_state, lent_att)):
        state[...] = jnp.zeros(state.shape, F32)
        state[0:1] = jnp.full((1, state.shape[1]), -jnp.inf, F32)
        total[...] = jnp.zeros(total.shape, F32)
    stats_out[...] = jnp.zeros(stats_out.shape, F32)
    dquery[...] = jnp.zeros(dquery.shape, F32)
    load_grads.wait()
    load_weight.wait()
    douts[mine] = dot(grads[...], weight[...], (1, 1)).astype(BF16)
    pl.semaphore_wait(pltpu.get_barrier_semaphore(), 23)

    def over(i, source, target):
        return remote(source, target, xsend.at[i], xrecv.at[i], place.partner)

    query_copy = over(0, queries.at[mine], queries.at[theirs])
    dout_copy = over(1, douts.at[mine], douts.at[theirs])
    att_copy = over(2, att_out, att_in)
    state_copy = over(3, state_out, state_in)
    stats_copy = over(4, stats_out, stats_in)
    dquery_copy = over(5, dquery_out, dquery_in)

    def window(col, hslot, part):
        return kv.at[col, part, tile_of(hslot)]

    def along_height(wslot, part):
        col = own + wslot
        for i, (there, to) in enumerate(neighbours(h)):
            slot = h - start(to)
            yield there, remote(
                window(col, place.hslot, part), window(col, slot, part),
                hsend.at[i, wslot, part], recv.at[col, slot, part], (place.f, to, place.w),
            )

    def along_width(hslot, part):
        for i, (there, to) in enumerate(neighbours(place.w)):
            col = own + place.w - start(to)
            yield there, remote(
                window(own + place.wslot, hslot, part), window(col, hslot, part),
                wsend.at[i, hslot, part], recv.at[col, hslot, part], (place.f, h, to),
            )

    def to_sibling(wslot, hslot, part):
        col = own + wslot
        yield True, remote(
            window(col, hslot, part), window(col, hslot, part), ssend.at[wslot, hslot, part],
            recv.at[col, hslot, part], place.sibling,
        )

    def take(plane, wslot, hslot, part):
        col = plane + wslot
        arrived(window(col, hslot, part), recv.at[col, hslot, part])

    def forward(plane, tiles, prob, prob_grad, col_max, state, total):
        width = state.shape[1]
        rows = [tile_of(hslot) for _, hslot in tiles]
        scores = [
            dot(kv[plane + wslot, 0, row], queries[:width], (1, 1))
            for (wslot, _), row in zip(tiles, rows)
        ]
        before = state[0:1]
        now = before
        for score in scores:
            now = jnp.maximum(now, jnp.max(score, axis=0, keepdims=True))
        shrink = jnp.exp2((before - now) * SCALE)
        row_sum = state[1:2] * shrink
        added = jnp.zeros((DIM, width), F32)
        for (wslot, hslot), row, score in zip(tiles, rows, scores):
            weights = jnp.exp2((score - now) * SCALE)
            row_sum += jnp.sum(weights, axis=0, keepdims=True)
            values = kv[plane + wslot, 1, row]
            prob[wslot, row] = weights
            prob_grad[wslot, row] = dot(values, douts[:width], (1, 1))
            col_max[wslot, hslot] = now
            added += dot(values, weights.astype(BF16), (0, 0))
        state[0:1] = now
        state[1:2] = row_sum
        total[...] = total[...] * shrink + added

    def forward_own(tiles):
        forward(kept, tiles, own_prob, own_grad, own_max, own_state, own_att)

    def forward_lent(tiles):
        forward(lent, tiles, lent_prob, lent_grad, lent_max, lent_state, lent_att)

    w0, h0 = wslots[0], hslots[0]
    begin(along_height(w0, 0))
    begin(along_width(h0, 1))
    begin(along_width(h0, 0))
    begin(along_height(w0, 1))
    begin(to_sibling(w0, h0, 0))
    begin(to_sibling(w0, h0, 1))
    query_copy.start()
    dout_copy.start()
    for wslot, hslot in zip(wslots[1:], hslots[1:]):
        take(own, w0, hslot, 0)
        begin(along_width(hslot, 0))
        begin(to_sibling(w0, hslot, 0))
        take(own, wslot, h0, 1)
        begin(along_height(wslot, 1))
        begin(to_sibling(wslot, h0, 1))
    for wslot, hslot in zip(wslots[1:], hslots[1:]):
        take(own, w0, hslot, 1)
        begin(to_sibling(w0, hslot, 1))
        take(own, wslot, h0, 0)
        begin(to_sibling(wslot, h0, 0))
    query_copy.wait()
    dout_copy.wait()
    steps = [[(w0, hslot) for hslot in hslots]]
    steps += [[(wslot, hslot) for wslot in wslots[1:]] for hslot in hslots]

    def from_corners(tiles):
        for part in range(2):
            for wslot, hslot in tiles:
                take(own, wslot, hslot, part)
                begin(to_sibling(wslot, hslot, part))

    for i in range(4):
        for wslot, hslot in steps[i]:
            for part in range(2):
                take(sib, wslot, hslot, part)
        if i < 3:
            forward_lent(steps[i])
            forward_own(steps[i])
        if 0 < i < 3:
            from_corners(steps[i + 1])
    forward_lent(steps[3])
    att_out[...] = lent_att[:, WIDE:].astype(BF16)
    state_out[...] = lent_state[:, WIDE:]
    att_copy.start()
    state_copy.start()
    forward_own(steps[3])

    att_copy.wait()
    state_copy.wait()
    shares = [
        (own_state[...], own_att[...]),
        (lent_state[:, :WIDE], lent_att[:, :WIDE]),
        (state_in[...], att_in[...].astype(F32)),
    ]
    row_max = jnp.maximum(jnp.maximum(shares[0][0][0:1], shares[1][0][0:1]), shares[2][0][0:1])
    row_sum = jnp.zeros((1, WIDE), F32)
    total = jnp.zeros((DIM, WIDE), F32)
    for state, partial in shares:
        shrink = jnp.exp2((state[0:1] - row_max) * SCALE)
        row_sum += state[1:2] * shrink
        total += partial * shrink
    inverse = 1.0 / row_sum
    attended_wide = (total * inverse).astype(BF16)
    attended = attended_wide[:, :ROWS]

    def weight_terms(side):
        def one(i, carry):
            columns = pl.ds(pl.multiple_of(side * 1536 + i * 512, 512), 512)
            term = dot(attended, grads[:, columns], (1, 0)).astype(BF16)
            for j in range(4):
                rows = pl.ds(pl.multiple_of(i * 512 + j * 128, 128), 128)
                terms[side, rows] = term[:, j * 128 : (j + 1) * 128]
            return carry

        lax.fori_loop(0, 3, one, 0)

    half_copy = remote(terms.at[1 - core], half, half_sem.at[0], half_sem.at[1], place.sibling)
    weight_terms(1 - core)
    half_copy.start()
    stats_out[0:1] = row_max
    stats_out[1:2] = inverse
    stats_out[2:3] = jnp.sum(
        jnp.transpose(douts[:WIDE].astype(F32)) * attended_wide.astype(F32), axis=0, keepdims=True
    )
    stats_copy.start()
    weight_terms(core)

    def backward(plane, wslot, prob, prob_grad, col_max, stats):
        width = prob.shape[2]
        added = jnp.zeros((DIM, width), F32)
        for hslot in range(3):
            rows = tile_of(hslot)
            share = jnp.exp2((col_max[wslot, hslot] - stats[0]) * SCALE) * stats[1]
            probability = prob[wslot, rows] * share
            score_grad = (probability * (prob_grad[wslot, rows] - stats[2])).astype(BF16)
            value_part = dot(probability.astype(BF16), douts[:width], (1, 0))
            key_part = dot(score_grad, queries[:width], (1, 0)) * ROOT
            parts[plane + wslot, 1, rows] = value_part.astype(BF16)
            parts[plane + wslot, 0, rows] = key_part.astype(BF16)
            added += dot(kv[plane + wslot, 0, rows], score_grad, (0, 0))
        dquery[:, :width] += added

    def swap_copy(wslot):
        return remote(
            parts.at[sib + wslot], swap.at[wslot], swap_send.at[wslot], swap_recv.at[wslot],
            place.sibling,
        )

    def own_column(wslot, carry):
        stats = [stats_out[i : i + 1] for i in range(3)]
        backward(kept, wslot, own_prob, own_grad, own_max, stats)
        pl.when(place.lends_own)(swap_copy(wslot).start)
        return carry

    lax.fori_loop(0, 3, own_column, 0)

    half_copy.wait()

    def piece_copy(chunk, k):
        to = place.plane_shift(k)
        return remote(
            half.at[piece_of(to, chunk)], pieces.at[chunk, ring], piece_send.at[chunk, to],
            piece_recv.at[chunk, ring], place.plane_chip(to),
        )

    def scatter(chunk):
        def add_half(piece, carry):
            rows = piece_of(piece, chunk)
            half[rows] = (terms[core, rows].astype(F32) + half[rows].astype(F32)).astype(BF16)
            return carry

        def start_piece(i, carry):
            piece_copy(chunk, far_first(i)).start()
            return carry

        lax.fori_loop(0, 16, add_half, 0)
        lax.fori_loop(0, 15, start_piece, 0)

    scatter(0)
    scatter(1)
    stats_copy.wait()

    def lent_column(wslot, carry):
        stats = [
            jnp.concatenate([stats_out[i : i + 1], stats_in[i : i + 1]], axis=1) for i in range(3)
        ]
        backward(lent, wslot, lent_prob, lent_grad, lent_max, stats)
        pl.when(place.lends_sib)(swap_copy(wslot).start)
        return carry

    lax.fori_loop(0, 3, lent_column, 0)
    dquery_out[...] = dquery[:, WIDE:]
    dquery_copy.start()

    def own_tile(wslot, hslot):
        rows = tile_of(hslot)
        outgoing[wslot, :, rows] = parts[own + wslot, :, rows].astype(F32) + swap[
            wslot, :, rows
        ].astype(F32)
        swap[wslot, :, rows] = outgoing[wslot, :, rows].astype(BF16)

    back = (1, 0, 2)

    def width_copy(i, to, hslot):
        return remote(
            swap.at[to - start(place.w), 0, tile_of(hslot)], wide.at[back[i], hslot],
            wide_send.at[i, hslot], wide_recv.at[back[i], hslot], (place.f, h, to),
        )

    def tall_copy(i, to, wslot):
        return remote(
            swap.at[wslot, 1, tile_of(to - start(h))], tall.at[back[i], wslot],
            tall_send.at[i, wslot], tall_recv.at[back[i], wslot], (place.f, to, place.w),
        )

    def own_rows(wslot, carry):
        arrived(swap.at[wslot], swap_recv.at[wslot])
        for hslot in range(3):
            own_tile(wslot, hslot)
        return carry

    lax.fori_loop(0, 3, own_rows, 0)

    def three(body):
        def one(slot, carry):
            body(slot)
            return carry

        lax.fori_loop(0, 3, one, 0)

    for i, (there, to) in enumerate(owners(place.w)):
        pl.when(there)(lambda: three(lambda slot: width_copy(i, to, slot).start()))
    for i, (there, to) in enumerate(owners(h)):
        pl.when(there)(lambda: three(lambda slot: tall_copy(i, to, slot).start()))

    def project(i, carry):
        columns = pl.ds(pl.multiple_of(i * 512, 512), 512)
        projected[:, columns] = dot(attended, weight[:, columns], (0, 0)).astype(BF16)
        return carry

    lax.fori_loop(0, 6, project, 0)
    store = pltpu.make_async_copy(projected, projected_hbm, store_sem)
    store.start()
    dquery_copy.wait()
    query_out[...] = (jnp.transpose(dquery[:, :WIDE] + dquery_in[...])[:ROWS] * ROOT).astype(BF16)

    def line_copy(chunk, k):
        to = lax.rem(h + k, 8)
        return remote(
            lines.at[chunk, h], lines.at[chunk, h], line_send.at[chunk, to],
            line_recv.at[chunk, h], (place.f, to, place.w),
        )

    def exchange(chunk):
        def add_piece(k, total):
            other = place.plane_shift(k)
            arrived(pieces.at[chunk, other], piece_recv.at[chunk, other])
            return total + pieces[chunk, other].astype(F32)

        def start_line(k, carry):
            line_copy(chunk, k).start()
            return carry

        total = lax.fori_loop(1, 16, add_piece, half[piece_of(ring, chunk)].astype(F32))
        lines[chunk, h] = total.astype(BF16)
        lax.fori_loop(1, 8, start_line, 0)
        return total

    totals = [exchange(0), exchange(1)]

    def add_wide(i, hslot):
        arrived(wide.at[i, hslot], wide_recv.at[i, hslot])
        outgoing[place.wslot, 0, tile_of(hslot)] += wide[i, hslot].astype(F32)

    def add_tall(i, wslot):
        arrived(tall.at[i, wslot], tall_recv.at[i, wslot])
        outgoing[wslot, 1, tile_of(place.hslot)] += tall[i, wslot].astype(F32)

    for i, (there, _w) in enumerate(neighbours(place.w)):
        pl.when(there)(lambda: three(lambda slot: add_wide(i, slot)))
    for i, (there, _h) in enumerate(neighbours(h)):
        pl.when(there)(lambda: three(lambda slot: add_tall(i, slot)))

    def height_copy(i, to):
        rows = tile_of(to - start(h))
        return remote(
            swap.at[place.wslot, 0, rows], high.at[back[i]], high_send.at[i],
            high_recv.at[back[i]], (place.f, to, place.w),
        )

    def side_copy(i, to):
        rows = tile_of(place.hslot)
        return remote(
            swap.at[to - start(place.w), 1, rows], side.at[back[i]], side_send.at[i],
            side_recv.at[back[i]], (place.f, h, to),
        )

    for i, (there, to) in enumerate(owners(h)):

        @pl.when(there)
        def _():
            rows = tile_of(to - start(h))
            swap[place.wslot, 0, rows] = outgoing[place.wslot, 0, rows].astype(BF16)
            height_copy(i, to).start()

    for i, (there, to) in enumerate(owners(place.w)):

        @pl.when(there)
        def _():
            rows = tile_of(place.hslot)
            wslot = to - start(place.w)
            swap[wslot, 1, rows] = outgoing[wslot, 1, rows].astype(BF16)
            side_copy(i, to).start()

    def full_copy(chunk, k):
        to = place.plane_shift(k)
        rows = piece_of(ring, chunk)
        return remote(
            full.at[core, rows], full.at[core, rows], full_send.at[chunk, to],
            full_recv.at[core, chunk, ring], place.plane_chip(to),
        )

    def pass_copy(chunk, piece):
        rows = piece_of(piece, chunk)
        return remote(
            full.at[core, rows], full.at[core, rows], pass_send.at[chunk, piece],
            full_recv.at[core, chunk, piece], place.sibling,
        )

    def spread(chunk):
        def add_line(k, total):
            other = lax.rem(h + k, 8)
            arrived(lines.at[chunk, other], line_recv.at[chunk, other])
            return total + lines[chunk, other].astype(F32)

        def start_full(i, carry):
            full_copy(chunk, far_first(i)).start()
            return carry

        total = lax.fori_loop(1, 8, add_line, totals[chunk])
        full[core, piece_of(ring, chunk)] = (total * (1.0 / 256.0)).astype(BF16)
        lax.fori_loop(0, 15, start_full, 0)
        pass_copy(chunk, ring).start()

    spread(0)
    spread(1)

    rows = tile_of(place.hslot)
    for i, (there, _h) in enumerate(neighbours(h)):

        @pl.when(there)
        def _():
            arrived(high.at[i], high_recv.at[i])
            outgoing[place.wslot, 0, rows] += high[i].astype(F32)

    for i, (there, _w) in enumerate(neighbours(place.w)):

        @pl.when(there)
        def _():
            arrived(side.at[i], side_recv.at[i])
            outgoing[place.wslot, 1, rows] += side[i].astype(F32)

    kv_out[...] = outgoing[place.wslot, :, rows].astype(BF16)

    for chunk in range(2):

        def pass_on(k, carry):
            other = place.plane_shift(k)
            arrived(full.at[core, piece_of(other, chunk)], full_recv.at[core, chunk, other])
            pass_copy(chunk, other).start()
            return carry

        lax.fori_loop(1, 16, pass_on, 0)

    def take_rest(piece, carry):
        for chunk in range(2):
            arrived(
                full.at[1 - core, piece_of(piece, chunk)], full_recv.at[1 - core, chunk, piece]
            )
        return carry

    lax.fori_loop(0, 16, take_rest, 0)

    def left_plane(k, carry):
        for chunk in range(2):
            piece_copy(chunk, k).wait_send()
            full_copy(chunk, k).wait_send()
        return carry

    lax.fori_loop(1, 16, left_plane, 0)

    def left_line(k, carry):
        for chunk in range(2):
            line_copy(chunk, k).wait_send()
        return carry

    lax.fori_loop(1, 8, left_line, 0)

    def left_pass(piece, carry):
        for chunk in range(2):
            pass_copy(chunk, piece).wait_send()
        return carry

    lax.fori_loop(0, 16, left_pass, 0)
    def left_column(slot, carry):
        swap_copy(slot).wait_send()
        for hslot in range(3):
            for part in range(2):
                finish(to_sibling(slot, hslot, part))
        finish(along_width(slot, 0))
        finish(along_height(slot, 1))
        return carry

    lax.fori_loop(0, 3, left_column, 0)
    finish(along_height(w0, 0))
    finish(along_width(h0, 1))
    for i, (there, to) in enumerate(owners(place.w)):
        pl.when(there)(lambda: three(lambda slot: width_copy(i, to, slot).wait_send()))
        pl.when(there)(side_copy(i, to).wait_send)
    for i, (there, to) in enumerate(owners(h)):
        pl.when(there)(lambda: three(lambda slot: tall_copy(i, to, slot).wait_send()))
        pl.when(there)(height_copy(i, to).wait_send)
    store.wait()


def write_kernel(
    projected, query, kv, full, projected_out, query_out, key_out, value_out, weight_out,
    rows, tiles, held, wide, load_sem, store_sem,
):
    pairs = [
        (full.at[0], held.at[0], None),
        (full.at[1], held.at[1], None),
        (query, tiles.at[0], query_out),
        (kv.at[0], tiles.at[1], key_out),
        (kv.at[1], tiles.at[2], value_out),
    ]
    for i in range(4):
        part = pl.ds(i * 48, 48)
        pairs.append((projected.at[part], rows.at[part], projected_out.at[part]))
    loads = [
        pltpu.make_async_copy(source, here, load_sem.at[i])
        for i, (source, here, _) in enumerate(pairs)
    ]
    for load in loads:
        load.start()
    stores = []
    for i, (_, here, target) in enumerate(pairs):
        loads[i].wait()
        if i < 2:
            for block in range(12):
                wide[i, :, block * 128 : (block + 1) * 128] = held[
                    i, block * 128 : (block + 1) * 128
                ].astype(F32)
            here, target = wide.at[i], weight_out.at[:, i * 1536 : (i + 1) * 1536]
        stores.append(pltpu.make_async_copy(here, target, store_sem.at[i]))
        stores[i].start()
    for store in stores:
        store.wait()


def body(queries, key_vectors, value_vectors, out_weight, projected_grad):
    vmem, dma = pltpu.VMEM, pltpu.SemaphoreType.DMA
    model = out_weight.shape[1]
    column = (2, 3 * ROWS, DIM)
    here, there = pl.BlockSpec(memory_space=pltpu.VMEM), pl.BlockSpec(memory_space=pl.ANY)
    tile = (ROWS, DIM)
    results = pl.pallas_call(
        kernel,
        out_shape=(
            jax.ShapeDtypeStruct((ROWS, model), BF16),
            jax.ShapeDtypeStruct(tile, BF16),
            jax.ShapeDtypeStruct((2, ROWS, DIM), BF16),
            jax.ShapeDtypeStruct((2, 1536, DIM), BF16),
        ),
        in_specs=[here, here, here, there, there],
        out_specs=[there, here, here, here],
        scratch_shapes=[
            vmem((6,) + column, BF16),
            vmem((2 * WIDE, DIM), BF16),
            vmem((2 * WIDE, DIM), BF16),
            vmem((3, 3 * ROWS, WIDE), F32),
            vmem((3, 3 * ROWS, WIDE), F32),
            vmem((3, 3, 1, WIDE), F32),
            vmem((3, 3 * ROWS, 2 * WIDE), F32),
            vmem((3, 3 * ROWS, 2 * WIDE), F32),
            vmem((3, 3, 1, 2 * WIDE), F32),
            vmem((8, WIDE), F32),
            vmem((8, 2 * WIDE), F32),
            vmem((DIM, WIDE), F32),
            vmem((DIM, 2 * WIDE), F32),
            vmem((DIM, WIDE), BF16),
            vmem((DIM, WIDE), BF16),
            vmem((8, WIDE), F32),
            vmem((8, WIDE), F32),
            vmem((8, WIDE), F32),
            vmem((8, WIDE), F32),
            vmem((DIM, 2 * WIDE), F32),
            vmem((DIM, WIDE), F32),
            vmem((DIM, WIDE), F32),
            vmem((ROWS, model), BF16),
            vmem((DIM, model), BF16),
            vmem((ROWS, model), BF16),
            vmem((2, 1536, DIM), BF16),
            vmem((1536, DIM), BF16),
            vmem((2, 16, 48, DIM), BF16),
            vmem((2, 8, 48, DIM), BF16),
            vmem((6,) + column, BF16),
            vmem((3,) + column, BF16),
            vmem((3,) + column, F32),
            vmem((3, 3) + tile, BF16),
            vmem((3, 3) + tile, BF16),
            vmem((3,) + tile, BF16),
            vmem((3,) + tile, BF16),
            dma((2,)),
            dma,
            dma((3, 3, 2)),
            dma((3, 3, 2)),
            dma((3, 3, 2)),
            dma((6, 3, 2)),
            dma((6,)),
            dma((6,)),
            dma((2,)),
            dma((2, 16)),
            dma((2, 16)),
            dma((2, 8)),
            dma((2, 8)),
            dma((2, 16)),
            dma((2, 16)),
            dma((2, 2, 16)),
            dma((3,)),
            dma((3,)),
            dma((3, 3)),
            dma((3, 3)),
            dma((3, 3)),
            dma((3, 3)),
            dma((3,)),
            dma((3,)),
            dma((3,)),
            dma((3,)),
        ],
        compiler_params=pltpu.CompilerParams(
            collective_id=0, has_side_effects=True, vmem_limit_bytes=LIMIT
        ),
        name="attention",
    )(
        queries.reshape(tile),
        key_vectors.reshape(tile),
        value_vectors.reshape(tile),
        out_weight,
        projected_grad.reshape(ROWS, model),
    )
    projected, grad_query, grad_key, grad_value, grad_out_weight = pl.pallas_call(
        write_kernel,
        out_shape=(
            jax.ShapeDtypeStruct((ROWS, model), BF16),
            jax.ShapeDtypeStruct(tile, BF16),
            jax.ShapeDtypeStruct(tile, BF16),
            jax.ShapeDtypeStruct(tile, BF16),
            jax.ShapeDtypeStruct((DIM, model), F32),
        ),
        in_specs=[there] * 4,
        out_specs=[there] * 5,
        scratch_shapes=[
            vmem((ROWS, model), BF16),
            vmem((3,) + tile, BF16),
            vmem((2, 1536, DIM), BF16),
            vmem((2, DIM, 1536), F32),
            dma((9,)),
            dma((9,)),
        ],
        compiler_params=pltpu.CompilerParams(vmem_limit_bytes=LIMIT),
        name="write",
    )(*results)
    return (
        projected.reshape(projected_grad.shape),
        grad_query.reshape(queries.shape),
        grad_key.reshape(queries.shape),
        grad_value.reshape(queries.shape),
        grad_out_weight,
    )


def solution(mesh):
    spec = P("frame", "height", "width", None)
    return jax.shard_map(
        body,
        mesh=mesh,
        in_specs=(spec, spec, spec, P(), spec),
        out_specs=(spec, spec, spec, spec, P()),
        check_vma=False,
    )
```

```python
import math

import jax
import jax.experimental.pallas as pl
import jax.experimental.pallas.tpu as pltpu
import jax.numpy as jnp
from jax import lax
from jax.sharding import PartitionSpec as P

MESH = pl.DeviceIdType.MESH
ROWS = 192
WIDE = 256
DIM = 128
LIMIT = 56 * 2**20
CHUNKS = 2
CHUNK = 96 // CHUNKS
BF16, F32 = jnp.bfloat16, jnp.float32
ROOT = 1.0 / math.sqrt(DIM)
SCALE = ROOT * math.log2(math.e)


FAR_FIRST = (10, 6, 9, 11, 14, 2, 5, 7, 8, 13, 15, 1, 3, 4, 12)


def wrap(index, size):
    return jnp.where(index >= size, index - size, index)


def step(index, bound):
    return jnp.where(index >= bound, 1, 0)


class Place:
    def __init__(self):
        self.f = lax.axis_index("frame")
        self.h = lax.axis_index("height")
        self.w = lax.axis_index("width")
        self.xlo = step(self.f, 2)
        self.core = self.f - 2 * self.xlo
        self.xhi = step(self.w, 4)
        self.y = self.w - 4 * self.xhi
        self.sibling = (self.xlo * 2 + 1 - self.core, self.h, self.w)
        self.partner = ((1 - self.xlo) * 2 + self.core, self.h, self.w)
        x = 2 * self.xhi + self.xlo
        self.xs = [x] + [wrap(x + d, 4) for d in (1, 2, 3)]
        self.ys = [self.y] + [wrap(self.y + d, 4) for d in (1, 2, 3)]
        self.hs = [self.h] + [wrap(self.h + d, 8) for d in range(1, 8)]
        self.frames = [2 * (at - 2 * step(at, 2)) + self.core for at in self.xs]
        self.widths = [4 * step(at, 2) for at in self.xs]
        self.ring = x * 4 + self.y
        self.own_plane = self.core
        self.sib_plane = 1 - self.core
        self.lent_plane = 1 - self.xlo
        self.lends_own = self.core != self.xlo
        self.lends_sib = self.core == self.xlo
        self.hslot = self.h - start(self.h)
        self.wslot = self.w - start(self.w)

    def plane_chip(self, k):
        return (self.frames[k // 4], self.h, self.widths[k // 4] + self.ys[k % 4])

    def plane_shift(self, k):
        return self.xs[k // 4] * 4 + self.ys[k % 4]


def start(index):
    return jnp.maximum(jnp.minimum(index - 1, 5), 0)


def neighbours(index):
    return (
        (index >= 1, index - 1),
        (index <= 6, index + 1),
        ((index == 2) | (index == 5), 7 * step(index, 5)),
    )


def owners(index):
    return (
        (index >= 1, index - 1),
        (index <= 6, index + 1),
        ((index == 0) | (index == 7), 2 + 3 * step(index, 7)),
    )


def remote(src, dst, send_sem, recv_sem, target):
    return pltpu.make_async_remote_copy(
        src_ref=src,
        dst_ref=dst,
        send_sem=send_sem,
        recv_sem=recv_sem,
        device_id=target,
        device_id_type=MESH,
    )


def arrived(ref, sem):
    pltpu.make_async_copy(ref, ref, sem).wait()


def greet_all(place):
    barrier = pltpu.get_barrier_semaphore()

    def greet(target):
        pl.semaphore_signal(barrier, inc=1, device_id=target, device_id_type=MESH)

    for k in (4, 3, 5, 2, 6):
        greet((place.f, place.hs[k], place.w))
    for k in FAR_FIRST:
        greet(place.plane_chip(k))
    for k in (1, 7):
        greet((place.f, place.hs[k], place.w))
    greet(place.sibling)


def begin(copies):
    for there, copy in copies:
        if there is True:
            copy.start()
        else:
            pl.when(there)(copy.start)


def finish(copies):
    for there, copy in copies:
        if there is True:
            copy.wait_send()
        else:
            pl.when(there)(copy.wait_send)


def tile_of(hslot):
    return pl.ds(pl.multiple_of(hslot * ROWS, ROWS), ROWS)


def piece_of(index, chunk):
    return pl.ds(pl.multiple_of(index * 96 + chunk * CHUNK, CHUNK), CHUNK)


def dot(left, right, over):
    return lax.dot_general(left, right, ((over[:1], over[1:]), ((), ())), preferred_element_type=F32)


def kernel(
    q_ref, k_ref, v_ref, weight_hbm, grad_hbm,
    projected_hbm, query_out, kv_out, full_hbm,
    kv, queries, douts, own_prob, own_grad, own_max, their_prob, their_grad, their_max,
    own_state, their_state, own_att, their_att, att_out, att_in, state_in, att_mine, att_sib,
    stats_out, stats_in, dquery, dquery_out, dquery_in,
    grads, grads_in, weight, projected,
    terms, half, pieces, lines, full,
    parts, swap, outgoing, wide, tall, high, side,
    load_sem, store_sem,
    hsend, wsend, ssend, recv, xsend, xrecv,
    half_sem, piece_send, piece_recv, line_send, line_recv, full_send, pass_send, full_recv,
    swap_send, swap_recv, wide_send, wide_recv, tall_send, tall_recv,
    high_send, high_recv, side_send, side_recv,
):
    place = Place()
    core, ring, h = place.core, place.ring, place.h
    own, sib, lent = place.own_plane * 3, place.sib_plane * 3, place.lent_plane * 3
    kept = 3 - lent
    hslots = (place.hslot, wrap(place.hslot + 1, 3), wrap(place.hslot + 2, 3))
    wslots = (place.wslot, wrap(place.wslot + 1, 3), wrap(place.wslot + 2, 3))
    mine, theirs = pl.ds(0, ROWS), pl.ds(WIDE, ROWS)

    greet_all(place)
    load_grads = pltpu.make_async_copy(grad_hbm, grads, load_sem.at[0])
    load_weight = pltpu.make_async_copy(weight_hbm, weight, load_sem.at[1])
    load_grads.start()
    load_weight.start()
    kv[own + place.wslot, 0, tile_of(place.hslot)] = k_ref[...]
    kv[own + place.wslot, 1, tile_of(place.hslot)] = v_ref[...]
    queries[mine] = q_ref[...]
    for first in (ROWS, WIDE + ROWS):
        queries[first : first + WIDE - ROWS] = jnp.zeros((WIDE - ROWS, DIM), BF16)
        douts[first : first + WIDE - ROWS] = jnp.zeros((WIDE - ROWS, DIM), BF16)
    for state, total in ((own_state, own_att), (their_state, their_att)):
        state[...] = jnp.zeros(state.shape, F32)
        state[0:1] = jnp.full((1, state.shape[1]), -jnp.inf, F32)
        total[...] = jnp.zeros(total.shape, F32)
    stats_out[...] = jnp.zeros(stats_out.shape, F32)
    dquery[...] = jnp.zeros(dquery.shape, F32)
    load_grads.wait()
    load_weight.wait()
    douts[mine] = dot(grads[...], weight[...], (1, 1)).astype(BF16)
    pl.semaphore_wait(pltpu.get_barrier_semaphore(), 23)

    def over(i, source, target):
        return remote(source, target, xsend.at[i], xrecv.at[i], place.partner)

    query_copy = over(0, queries.at[mine], queries.at[theirs])
    dout_copy = over(1, douts.at[mine], douts.at[theirs])
    att_copy = over(2, att_out, att_in)
    state_copy = over(3, their_state, state_in)
    stats_copy = over(4, stats_out, stats_in)
    dquery_copy = over(5, dquery_out, dquery_in)

    def beside(i, source, target):
        return remote(source, target, half_sem.at[i], half_sem.at[2 + i], place.sibling)

    their_side = pl.ds(pl.multiple_of((1 - core) * 1536, 1536), 1536)
    grads_copy = beside(0, grads.at[:, their_side], grads_in)
    sib_copy = beside(1, att_mine, att_sib)

    def window(col, hslot, part):
        return kv.at[col, part, tile_of(hslot)]

    def along_height(wslot, part):
        col = own + wslot
        for i, (there, to) in enumerate(neighbours(h)):
            slot = h - start(to)
            yield there, remote(
                window(col, place.hslot, part), window(col, slot, part),
                hsend.at[i, wslot, part], recv.at[col, slot, part], (place.f, to, place.w),
            )

    def along_width(hslot, part):
        for i, (there, to) in enumerate(neighbours(place.w)):
            col = own + place.w - start(to)
            yield there, remote(
                window(own + place.wslot, hslot, part), window(col, hslot, part),
                wsend.at[i, hslot, part], recv.at[col, hslot, part], (place.f, h, to),
            )

    def to_sibling(wslot, hslot, part):
        col = own + wslot
        yield True, remote(
            window(col, hslot, part), window(col, hslot, part), ssend.at[wslot, hslot, part],
            recv.at[col, hslot, part], place.sibling,
        )

    def take(plane, wslot, hslot, part):
        col = plane + wslot
        arrived(window(col, hslot, part), recv.at[col, hslot, part])

    def forward(plane, base, first, tiles, prob, prob_grad, col_max, state, total):
        rows = [tile_of(hslot) for _, hslot in tiles]
        scores = [
            dot(kv[plane + wslot, 0, row], queries[first : first + WIDE], (1, 1))
            for (wslot, _), row in zip(tiles, rows)
        ]
        before = state[0:1]
        now = before
        for score in scores:
            now = jnp.maximum(now, jnp.max(score, axis=0, keepdims=True))
        shrink = jnp.exp2((before - now) * SCALE)
        row_sum = state[1:2] * shrink
        added = jnp.zeros((DIM, WIDE), F32)
        for (wslot, hslot), row, score in zip(tiles, rows, scores):
            weights = jnp.exp2((score - now) * SCALE)
            row_sum += jnp.sum(weights, axis=0, keepdims=True)
            values = kv[plane + wslot, 1, row]
            prob[base + wslot, row] = weights
            prob_grad[base + wslot, row] = dot(values, douts[first : first + WIDE], (1, 1))
            col_max[base + wslot, hslot] = now
            added += dot(values, weights.astype(BF16), (0, 0))
        state[0:1] = now
        state[1:2] = row_sum
        total[...] = total[...] * shrink + added

    def ours(plane, tiles):
        forward(plane, plane, 0, tiles, own_prob, own_grad, own_max, own_state, own_att)

    def theirs(tiles):
        forward(
            lent, 0, WIDE, tiles, their_prob, their_grad, their_max, their_state, their_att
        )

    def from_sibling(tiles):
        for wslot, hslot in tiles:
            for part in range(2):
                take(sib, wslot, hslot, part)

    w0, h0 = wslots[0], hslots[0]
    begin(along_height(w0, 0))
    begin(along_width(h0, 1))
    begin(along_width(h0, 0))
    begin(along_height(w0, 1))
    begin(to_sibling(w0, h0, 0))
    begin(to_sibling(w0, h0, 1))
    query_copy.start()
    dout_copy.start()
    grads_copy.start()
    for wslot, hslot in zip(wslots[1:], hslots[1:]):
        take(own, w0, hslot, 0)
        begin(along_width(hslot, 0))
        begin(to_sibling(w0, hslot, 0))
        take(own, wslot, h0, 1)
        begin(along_height(wslot, 1))
        begin(to_sibling(wslot, h0, 1))
    for wslot, hslot in zip(wslots[1:], hslots[1:]):
        take(own, w0, hslot, 1)
        begin(to_sibling(w0, hslot, 1))
        take(own, wslot, h0, 0)
        begin(to_sibling(wslot, h0, 0))
    steps = [[(w0, hslot) for hslot in hslots]]
    steps += [[(wslot, hslot) for wslot in wslots[1:]] for hslot in hslots]

    def from_corners(tiles):
        for part in range(2):
            for wslot, hslot in tiles:
                take(own, wslot, hslot, part)
                begin(to_sibling(wslot, hslot, part))

    ours(own, steps[0])
    query_copy.wait()
    dout_copy.wait()
    from_sibling(steps[0])
    theirs(steps[0])
    ours(sib, steps[0])
    ours(own, steps[1])
    from_sibling(steps[1])
    theirs(steps[1])
    ours(sib, steps[1])
    from_corners(steps[2])
    ours(own, steps[2])
    from_corners(steps[3])
    from_sibling(steps[2])
    theirs(steps[2])
    ours(sib, steps[2])
    ours(own, steps[3])
    from_sibling(steps[3])
    theirs(steps[3])
    att_out[...] = their_att[...].astype(BF16)
    att_copy.start()
    state_copy.start()
    ours(sib, steps[3])

    grads_copy.wait()
    att_copy.wait()
    state_copy.wait()
    before = own_state[0:1]
    row_max = jnp.maximum(before, state_in[0:1])
    shrink = jnp.exp2((before - row_max) * SCALE)
    shrink_in = jnp.exp2((state_in[0:1] - row_max) * SCALE)
    inverse = 1.0 / (own_state[1:2] * shrink + state_in[1:2] * shrink_in)
    attended_wide = (
        (own_att[...] * shrink + att_in[...].astype(F32) * shrink_in) * inverse
    ).astype(BF16)
    att_mine[...] = attended_wide
    sib_copy.start()
    attended = attended_wide[:, :ROWS]
    stats_out[0:1] = row_max
    stats_out[1:2] = inverse
    stats_out[2:3] = jnp.sum(
        jnp.transpose(douts[:WIDE].astype(F32)) * attended_wide.astype(F32), axis=0, keepdims=True
    )
    stats_copy.start()
    for i in range(3):
        columns = pl.ds(pl.multiple_of(core * 1536 + i * 512, 512), 512)
        terms[i] = dot(attended, grads[:, columns], (1, 0))
    sib_copy.wait()
    for i in range(3):
        term = terms[i] + dot(
            att_sib[:, :ROWS], grads_in[:, i * 512 : (i + 1) * 512], (1, 0)
        )
        for j in range(4):
            half[i * 512 + j * 128 : i * 512 + (j + 1) * 128] = term[
                :, j * 128 : (j + 1) * 128
            ].astype(BF16)

    def backward(plane, wslot, both):
        added = jnp.zeros((DIM, 2 * WIDE if both else WIDE), F32)
        for hslot in range(3):
            rows = tile_of(hslot)
            held = [(own_prob, own_grad, own_max, stats_out, plane + wslot)]
            if both:
                held.append((their_prob, their_grad, their_max, stats_in, wslot))
            shares, score_grads = [], []
            for prob, prob_grad, col_max, stats, col in held:
                share = jnp.exp2((col_max[col, hslot] - stats[0:1]) * SCALE) * stats[1:2]
                probability = prob[col, rows] * share
                shares.append(probability.astype(BF16))
                score_grads.append(
                    (probability * (prob_grad[col, rows] - stats[2:3])).astype(BF16)
                )
            share = jnp.concatenate(shares, axis=1) if both else shares[0]
            score_grad = jnp.concatenate(score_grads, axis=1) if both else score_grads[0]
            width = added.shape[1]
            value_part = dot(share, douts[:width], (1, 0))
            key_part = dot(score_grad, queries[:width], (1, 0)) * ROOT
            parts[plane + wslot, 1, rows] = value_part.astype(BF16)
            parts[plane + wslot, 0, rows] = key_part.astype(BF16)
            added += dot(kv[plane + wslot, 0, rows], score_grad, (0, 0))
        dquery[:, : added.shape[1]] += added

    def swap_copy(wslot):
        return remote(
            parts.at[sib + wslot], swap.at[wslot], swap_send.at[wslot], swap_recv.at[wslot],
            place.sibling,
        )

    def own_column(wslot, carry):
        backward(kept, wslot, False)
        pl.when(place.lends_own)(swap_copy(wslot).start)
        return carry

    def piece_copy(chunk, k):
        to = place.plane_shift(k)
        return remote(
            half.at[piece_of(to, chunk)], pieces.at[chunk, ring], piece_send.at[chunk, to],
            piece_recv.at[chunk, ring], place.plane_chip(k),
        )

    for chunk in range(CHUNKS):

        for k in FAR_FIRST:
            piece_copy(chunk, k).start()
    lax.fori_loop(0, 3, own_column, 0)
    stats_copy.wait()

    def lent_column(wslot, carry):
        backward(lent, wslot, True)
        pl.when(place.lends_sib)(swap_copy(wslot).start)
        return carry

    lax.fori_loop(0, 3, lent_column, 0)
    dquery_out[...] = dquery[:, WIDE:]
    dquery_copy.start()

    def own_tile(wslot, hslot):
        rows = tile_of(hslot)
        outgoing[wslot, :, rows] = parts[own + wslot, :, rows].astype(F32) + swap[
            wslot, :, rows
        ].astype(F32)
        swap[wslot, :, rows] = outgoing[wslot, :, rows].astype(BF16)

    back = (1, 0, 2)

    def width_copy(i, to, hslot):
        return remote(
            swap.at[to - start(place.w), 0, tile_of(hslot)], wide.at[back[i], hslot],
            wide_send.at[i, hslot], wide_recv.at[back[i], hslot], (place.f, h, to),
        )

    def tall_copy(i, to, wslot):
        return remote(
            swap.at[wslot, 1, tile_of(to - start(h))], tall.at[back[i], wslot],
            tall_send.at[i, wslot], tall_recv.at[back[i], wslot], (place.f, to, place.w),
        )

    def own_rows(wslot, carry):
        arrived(swap.at[wslot], swap_recv.at[wslot])
        for hslot in range(3):
            own_tile(wslot, hslot)
        return carry

    lax.fori_loop(0, 3, own_rows, 0)

    def three(body):
        def one(slot, carry):
            body(slot)
            return carry

        lax.fori_loop(0, 3, one, 0)

    for i, (there, to) in enumerate(owners(place.w)):
        pl.when(there)(lambda: three(lambda slot: width_copy(i, to, slot).start()))
    for i, (there, to) in enumerate(owners(h)):
        pl.when(there)(lambda: three(lambda slot: tall_copy(i, to, slot).start()))

    def project(i, carry):
        columns = pl.ds(pl.multiple_of(i * 512, 512), 512)
        projected[:, columns] = dot(attended, weight[:, columns], (0, 0)).astype(BF16)
        return carry

    lax.fori_loop(0, 6, project, 0)
    store = pltpu.make_async_copy(projected, projected_hbm, store_sem.at[0])
    store.start()
    dquery_copy.wait()
    query_out[...] = (jnp.transpose(dquery[:, :WIDE] + dquery_in[...])[:ROWS] * ROOT).astype(BF16)

    def line_copy(chunk, k):
        to = place.hs[k]
        return remote(
            lines.at[chunk, h], lines.at[chunk, h], line_send.at[chunk, to],
            line_recv.at[chunk, h], (place.f, to, place.w),
        )

    def exchange(chunk):
        total = half[piece_of(ring, chunk)].astype(F32)
        for k in range(1, 16):
            other = place.plane_shift(k)
            arrived(pieces.at[chunk, other], piece_recv.at[chunk, other])
            total = total + pieces[chunk, other].astype(F32)
        lines[chunk, h] = total.astype(BF16)
        for k in (4, 3, 5, 2, 6, 1, 7):
            line_copy(chunk, k).start()
        return total

    totals = [exchange(chunk) for chunk in range(CHUNKS)]

    def add_wide(i, hslot):
        arrived(wide.at[i, hslot], wide_recv.at[i, hslot])
        outgoing[place.wslot, 0, tile_of(hslot)] += wide[i, hslot].astype(F32)

    def add_tall(i, wslot):
        arrived(tall.at[i, wslot], tall_recv.at[i, wslot])
        outgoing[wslot, 1, tile_of(place.hslot)] += tall[i, wslot].astype(F32)

    for i, (there, _w) in enumerate(neighbours(place.w)):
        pl.when(there)(lambda: three(lambda slot: add_wide(i, slot)))
    for i, (there, _h) in enumerate(neighbours(h)):
        pl.when(there)(lambda: three(lambda slot: add_tall(i, slot)))

    def height_copy(i, to):
        rows = tile_of(to - start(h))
        return remote(
            swap.at[place.wslot, 0, rows], high.at[back[i]], high_send.at[i],
            high_recv.at[back[i]], (place.f, to, place.w),
        )

    def side_copy(i, to):
        rows = tile_of(place.hslot)
        return remote(
            swap.at[to - start(place.w), 1, rows], side.at[back[i]], side_send.at[i],
            side_recv.at[back[i]], (place.f, h, to),
        )

    for i, (there, to) in enumerate(owners(h)):

        @pl.when(there)
        def _():
            rows = tile_of(to - start(h))
            swap[place.wslot, 0, rows] = outgoing[place.wslot, 0, rows].astype(BF16)
            height_copy(i, to).start()

    for i, (there, to) in enumerate(owners(place.w)):

        @pl.when(there)
        def _():
            rows = tile_of(place.hslot)
            wslot = to - start(place.w)
            swap[wslot, 1, rows] = outgoing[wslot, 1, rows].astype(BF16)
            side_copy(i, to).start()

    def full_copy(chunk, k):
        to = place.plane_shift(k)
        rows = piece_of(ring, chunk)
        return remote(
            full.at[core, rows], full.at[core, rows], full_send.at[chunk, to],
            full_recv.at[core, chunk, ring], place.plane_chip(k),
        )

    def pass_copy(chunk, piece):
        rows = piece_of(piece, chunk)
        return remote(
            full.at[core, rows], full.at[core, rows], pass_send.at[chunk, piece],
            full_recv.at[core, chunk, piece], place.sibling,
        )

    def spread(chunk):
        total = totals[chunk]
        for k in range(1, 8):
            other = place.hs[k]
            arrived(lines.at[chunk, other], line_recv.at[chunk, other])
            total = total + lines[chunk, other].astype(F32)
        full[core, piece_of(ring, chunk)] = (total * (1.0 / 256.0)).astype(BF16)
        for k in FAR_FIRST:
            full_copy(chunk, k).start()
        pass_copy(chunk, ring).start()

    for chunk in range(CHUNKS):
        spread(chunk)

    for chunk in range(CHUNKS):
        for k in range(1, 16):
            piece_copy(chunk, k).wait_send()
        for k in range(1, 8):
            line_copy(chunk, k).wait_send()

    def left_column(slot, carry):
        swap_copy(slot).wait_send()
        for hslot in range(3):
            for part in range(2):
                finish(to_sibling(slot, hslot, part))
        finish(along_width(slot, 0))
        finish(along_height(slot, 1))
        return carry

    lax.fori_loop(0, 3, left_column, 0)
    finish(along_height(w0, 0))
    finish(along_width(h0, 1))
    for i, (there, to) in enumerate(owners(place.w)):
        pl.when(there)(lambda: three(lambda slot: width_copy(i, to, slot).wait_send()))
    for i, (there, to) in enumerate(owners(h)):
        pl.when(there)(lambda: three(lambda slot: tall_copy(i, to, slot).wait_send()))

    rows = tile_of(place.hslot)
    for i, (there, _h) in enumerate(neighbours(h)):

        @pl.when(there)
        def _():
            arrived(high.at[i], high_recv.at[i])
            outgoing[place.wslot, 0, rows] += high[i].astype(F32)

    for i, (there, _w) in enumerate(neighbours(place.w)):

        @pl.when(there)
        def _():
            arrived(side.at[i], side_recv.at[i])
            outgoing[place.wslot, 1, rows] += side[i].astype(F32)

    kv_out[...] = outgoing[place.wslot, :, rows].astype(BF16)

    for chunk in range(CHUNKS):

        for k in range(1, 16):
            other = place.plane_shift(k)
            arrived(full.at[core, piece_of(other, chunk)], full_recv.at[core, chunk, other])
            pass_copy(chunk, other).start()
    store_half = pltpu.make_async_copy(full.at[core], full_hbm.at[core], store_sem.at[1])
    store_half.start()

    def take_rest(piece, carry):
        for chunk in range(CHUNKS):
            arrived(
                full.at[1 - core, piece_of(piece, chunk)], full_recv.at[1 - core, chunk, piece]
            )
        return carry

    lax.fori_loop(0, 16, take_rest, 0)
    store_rest = pltpu.make_async_copy(
        full.at[1 - core], full_hbm.at[1 - core], store_sem.at[2]
    )
    store_rest.start()

    for chunk in range(CHUNKS):
        for k in range(1, 16):
            full_copy(chunk, k).wait_send()

    def left_pass(piece, carry):
        for chunk in range(CHUNKS):
            pass_copy(chunk, piece).wait_send()
        return carry

    lax.fori_loop(0, 16, left_pass, 0)
    for i, (there, to) in enumerate(owners(place.w)):
        pl.when(there)(side_copy(i, to).wait_send)
    for i, (there, to) in enumerate(owners(h)):
        pl.when(there)(height_copy(i, to).wait_send)
    store.wait()
    store_half.wait()
    store_rest.wait()


def write_kernel(
    projected, query, kv, full, projected_out, query_out, key_out, value_out, weight_out,
    rows, tiles, held, wide, load_sem, store_sem,
):
    pairs = [
        (full.at[0], held.at[0], None),
        (full.at[1], held.at[1], None),
        (query, tiles.at[0], query_out),
        (kv.at[0], tiles.at[1], key_out),
        (kv.at[1], tiles.at[2], value_out),
    ]
    for i in range(4):
        part = pl.ds(i * 48, 48)
        pairs.append((projected.at[part], rows.at[part], projected_out.at[part]))
    loads = [
        pltpu.make_async_copy(source, here, load_sem.at[i])
        for i, (source, here, _) in enumerate(pairs)
    ]
    for load in loads:
        load.start()
    stores = []
    for i, (_, here, target) in enumerate(pairs):
        loads[i].wait()
        if i < 2:
            for block in range(12):
                wide[i, :, block * 128 : (block + 1) * 128] = held[
                    i, block * 128 : (block + 1) * 128
                ].astype(F32)
            here, target = wide.at[i], weight_out.at[:, i * 1536 : (i + 1) * 1536]
        stores.append(pltpu.make_async_copy(here, target, store_sem.at[i]))
        stores[i].start()
    for store in stores:
        store.wait()


def body(queries, key_vectors, value_vectors, out_weight, projected_grad):
    vmem, dma = pltpu.VMEM, pltpu.SemaphoreType.DMA
    model = out_weight.shape[1]
    column = (2, 3 * ROWS, DIM)
    here, there = pl.BlockSpec(memory_space=pltpu.VMEM), pl.BlockSpec(memory_space=pl.ANY)
    tile = (ROWS, DIM)
    results = pl.pallas_call(
        kernel,
        out_shape=(
            jax.ShapeDtypeStruct((ROWS, model), BF16),
            jax.ShapeDtypeStruct(tile, BF16),
            jax.ShapeDtypeStruct((2, ROWS, DIM), BF16),
            jax.ShapeDtypeStruct((2, 1536, DIM), BF16),
        ),
        in_specs=[here, here, here, there, there],
        out_specs=[there, here, here, there],
        scratch_shapes=[
            vmem((6,) + column, BF16),
            vmem((2 * WIDE, DIM), BF16),
            vmem((2 * WIDE, DIM), BF16),
            vmem((6, 3 * ROWS, WIDE), F32),
            vmem((6, 3 * ROWS, WIDE), F32),
            vmem((6, 3, 1, WIDE), F32),
            vmem((3, 3 * ROWS, WIDE), F32),
            vmem((3, 3 * ROWS, WIDE), F32),
            vmem((3, 3, 1, WIDE), F32),
            vmem((8, WIDE), F32),
            vmem((8, WIDE), F32),
            vmem((DIM, WIDE), F32),
            vmem((DIM, WIDE), F32),
            vmem((DIM, WIDE), BF16),
            vmem((DIM, WIDE), BF16),
            vmem((8, WIDE), F32),
            vmem((DIM, WIDE), BF16),
            vmem((DIM, WIDE), BF16),
            vmem((8, WIDE), F32),
            vmem((8, WIDE), F32),
            vmem((DIM, 2 * WIDE), F32),
            vmem((DIM, WIDE), F32),
            vmem((DIM, WIDE), F32),
            vmem((ROWS, model), BF16),
            vmem((ROWS, 1536), BF16),
            vmem((DIM, model), BF16),
            vmem((ROWS, model), BF16),
            vmem((3, DIM, 512), F32),
            vmem((1536, DIM), BF16),
            vmem((CHUNKS, 16, CHUNK, DIM), BF16),
            vmem((CHUNKS, 8, CHUNK, DIM), BF16),
            vmem((2, 1536, DIM), BF16),
            vmem((6,) + column, BF16),
            vmem((3,) + column, BF16),
            vmem((3,) + column, F32),
            vmem((3, 3) + tile, BF16),
            vmem((3, 3) + tile, BF16),
            vmem((3,) + tile, BF16),
            vmem((3,) + tile, BF16),
            dma((2,)),
            dma((3,)),
            dma((3, 3, 2)),
            dma((3, 3, 2)),
            dma((3, 3, 2)),
            dma((6, 3, 2)),
            dma((6,)),
            dma((6,)),
            dma((4,)),
            dma((CHUNKS, 16)),
            dma((CHUNKS, 16)),
            dma((CHUNKS, 8)),
            dma((CHUNKS, 8)),
            dma((CHUNKS, 16)),
            dma((CHUNKS, 16)),
            dma((2, CHUNKS, 16)),
            dma((3,)),
            dma((3,)),
            dma((3, 3)),
            dma((3, 3)),
            dma((3, 3)),
            dma((3, 3)),
            dma((3,)),
            dma((3,)),
            dma((3,)),
            dma((3,)),
        ],
        compiler_params=pltpu.CompilerParams(
            collective_id=0, has_side_effects=True, vmem_limit_bytes=LIMIT
        ),
        name="attention",
    )(
        queries.reshape(tile),
        key_vectors.reshape(tile),
        value_vectors.reshape(tile),
        out_weight,
        projected_grad.reshape(ROWS, model),
    )
    projected, grad_query, grad_key, grad_value, grad_out_weight = pl.pallas_call(
        write_kernel,
        out_shape=(
            jax.ShapeDtypeStruct((ROWS, model), BF16),
            jax.ShapeDtypeStruct(tile, BF16),
            jax.ShapeDtypeStruct(tile, BF16),
            jax.ShapeDtypeStruct(tile, BF16),
            jax.ShapeDtypeStruct((DIM, model), F32),
        ),
        in_specs=[there] * 4,
        out_specs=[there] * 5,
        scratch_shapes=[
            vmem((ROWS, model), BF16),
            vmem((3,) + tile, BF16),
            vmem((2, 1536, DIM), BF16),
            vmem((2, DIM, 1536), F32),
            dma((9,)),
            dma((9,)),
        ],
        compiler_params=pltpu.CompilerParams(vmem_limit_bytes=LIMIT),
        name="write",
    )(*results)
    return (
        projected.reshape(projected_grad.shape),
        grad_query.reshape(queries.shape),
        grad_key.reshape(queries.shape),
        grad_value.reshape(queries.shape),
        grad_out_weight,
    )


def solution(mesh):
    spec = P("frame", "height", "width", None)
    return jax.shard_map(
        body,
        mesh=mesh,
        in_specs=(spec, spec, spec, P(), spec),
        out_specs=(spec, spec, spec, spec, P()),
        check_vma=False,
    )
```

```python
import math

import jax
import jax.experimental.pallas as pl
import jax.experimental.pallas.tpu as pltpu
import jax.numpy as jnp
from jax import lax
from jax.sharding import PartitionSpec as P

MESH = pl.DeviceIdType.MESH
ROWS = 192
WIDE = 256
DIM = 128
LIMIT = 56 * 2**20
CHUNKS = 2
CHUNK = 96 // CHUNKS
BF16, F32 = jnp.bfloat16, jnp.float32
ROOT = 1.0 / math.sqrt(DIM)
SCALE = ROOT * math.log2(math.e)


FAR_FIRST = (10, 6, 9, 11, 14, 2, 5, 7, 8, 13, 15, 1, 3, 4, 12)


def wrap(index, size):
    return jnp.where(index >= size, index - size, index)


def step(index, bound):
    return jnp.where(index >= bound, 1, 0)


class Place:
    def __init__(self):
        self.f = lax.axis_index("frame")
        self.h = lax.axis_index("height")
        self.w = lax.axis_index("width")
        self.xlo = step(self.f, 2)
        self.core = self.f - 2 * self.xlo
        self.xhi = step(self.w, 4)
        self.y = self.w - 4 * self.xhi
        self.sibling = (self.xlo * 2 + 1 - self.core, self.h, self.w)
        self.partner = ((1 - self.xlo) * 2 + self.core, self.h, self.w)
        x = 2 * self.xhi + self.xlo
        self.xs = [x] + [wrap(x + d, 4) for d in (1, 2, 3)]
        self.ys = [self.y] + [wrap(self.y + d, 4) for d in (1, 2, 3)]
        self.hs = [self.h] + [wrap(self.h + d, 8) for d in range(1, 8)]
        self.frames = [2 * (at - 2 * step(at, 2)) + self.core for at in self.xs]
        self.widths = [4 * step(at, 2) for at in self.xs]
        self.ring = x * 4 + self.y
        self.own_plane = self.core
        self.sib_plane = 1 - self.core
        self.lent_plane = 1 - self.xlo
        self.lends_own = self.core != self.xlo
        self.lends_sib = self.core == self.xlo
        self.hslot = self.h - start(self.h)
        self.wslot = self.w - start(self.w)

    def plane_chip(self, k):
        return (self.frames[k // 4], self.h, self.widths[k // 4] + self.ys[k % 4])

    def plane_shift(self, k):
        return self.xs[k // 4] * 4 + self.ys[k % 4]


def start(index):
    return jnp.maximum(jnp.minimum(index - 1, 5), 0)


def neighbours(index):
    return (
        (index >= 1, index - 1),
        (index <= 6, index + 1),
        ((index == 2) | (index == 5), 7 * step(index, 5)),
    )


def owners(index):
    return (
        (index >= 1, index - 1),
        (index <= 6, index + 1),
        ((index == 0) | (index == 7), 2 + 3 * step(index, 7)),
    )


def remote(src, dst, send_sem, recv_sem, target):
    return pltpu.make_async_remote_copy(
        src_ref=src,
        dst_ref=dst,
        send_sem=send_sem,
        recv_sem=recv_sem,
        device_id=target,
        device_id_type=MESH,
    )


def arrived(ref, sem):
    pltpu.make_async_copy(ref, ref, sem).wait()


def greet_all(place):
    barrier = pltpu.get_barrier_semaphore()

    def greet(target):
        pl.semaphore_signal(barrier, inc=1, device_id=target, device_id_type=MESH)

    for k in (4, 3, 5, 2, 6):
        greet((place.f, place.hs[k], place.w))
    for k in FAR_FIRST:
        greet(place.plane_chip(k))
    for k in (1, 7):
        greet((place.f, place.hs[k], place.w))
    greet(place.sibling)


def begin(copies):
    for there, copy in copies:
        if there is True:
            copy.start()
        else:
            pl.when(there)(copy.start)


def finish(copies):
    for there, copy in copies:
        if there is True:
            copy.wait_send()
        else:
            pl.when(there)(copy.wait_send)


def tile_of(hslot):
    return pl.ds(pl.multiple_of(hslot * ROWS, ROWS), ROWS)


def piece_of(index, chunk):
    return pl.ds(pl.multiple_of((chunk * 16 + index) * CHUNK, CHUNK), CHUNK)


def group_of(index, chunk):
    return pl.ds(pl.multiple_of((chunk * 16 + index * 4) * CHUNK, 4 * CHUNK), 4 * CHUNK)


def dot(left, right, over):
    return lax.dot_general(left, right, ((over[:1], over[1:]), ((), ())), preferred_element_type=F32)


def kernel(
    q_ref, k_ref, v_ref, weight_hbm, grad_hbm,
    projected_hbm, query_out, kv_out, full_hbm,
    kv, queries, douts, own_prob, own_grad, own_max, their_prob, their_grad, their_max,
    own_state, their_state, own_att, their_att, att_out, att_in, state_in, att_mine, att_sib,
    stats_out, stats_in, dquery, dquery_out, dquery_in,
    grads, grads_in, weight, projected,
    terms, half, pieces, lines, full,
    parts, swap, outgoing, wide, tall, high, side,
    load_sem, store_sem,
    hsend, wsend, ssend, recv, xsend, xrecv,
    half_sem, piece_send, piece_recv, line_send, line_recv, full_send, pass_send, pass_recv, full_recv,
    swap_send, swap_recv, wide_send, wide_recv, tall_send, tall_recv,
    high_send, high_recv, side_send, side_recv,
):
    place = Place()
    core, ring, h = place.core, place.ring, place.h
    own, sib, lent = place.own_plane * 3, place.sib_plane * 3, place.lent_plane * 3
    kept = 3 - lent
    hslots = (place.hslot, wrap(place.hslot + 1, 3), wrap(place.hslot + 2, 3))
    wslots = (place.wslot, wrap(place.wslot + 1, 3), wrap(place.wslot + 2, 3))
    mine, theirs = pl.ds(0, ROWS), pl.ds(WIDE, ROWS)

    greet_all(place)
    load_grads = pltpu.make_async_copy(grad_hbm, grads, load_sem.at[0])
    load_weight = pltpu.make_async_copy(weight_hbm, weight, load_sem.at[1])
    load_grads.start()
    load_weight.start()
    kv[own + place.wslot, 0, tile_of(place.hslot)] = k_ref[...]
    kv[own + place.wslot, 1, tile_of(place.hslot)] = v_ref[...]
    queries[mine] = q_ref[...]
    for first in (ROWS, WIDE + ROWS):
        queries[first : first + WIDE - ROWS] = jnp.zeros((WIDE - ROWS, DIM), BF16)
        douts[first : first + WIDE - ROWS] = jnp.zeros((WIDE - ROWS, DIM), BF16)
    for state, total in ((own_state, own_att), (their_state, their_att)):
        state[...] = jnp.zeros(state.shape, F32)
        state[0:1] = jnp.full((1, state.shape[1]), -jnp.inf, F32)
        total[...] = jnp.zeros(total.shape, F32)
    stats_out[...] = jnp.zeros(stats_out.shape, F32)
    dquery[...] = jnp.zeros(dquery.shape, F32)
    load_grads.wait()
    load_weight.wait()
    douts[mine] = dot(grads[...], weight[...], (1, 1)).astype(BF16)
    pl.semaphore_wait(pltpu.get_barrier_semaphore(), 23)

    def over(i, source, target):
        return remote(source, target, xsend.at[i], xrecv.at[i], place.partner)

    query_copy = over(0, queries.at[mine], queries.at[theirs])
    dout_copy = over(1, douts.at[mine], douts.at[theirs])
    att_copy = over(2, att_out, att_in)
    state_copy = over(3, their_state, state_in)
    stats_copy = over(4, stats_out, stats_in)
    dquery_copy = over(5, dquery_out, dquery_in)

    def beside(i, source, target):
        return remote(source, target, half_sem.at[i], half_sem.at[2 + i], place.sibling)

    their_side = pl.ds(pl.multiple_of((1 - core) * 1536, 1536), 1536)
    grads_copy = beside(0, grads.at[:, their_side], grads_in)
    sib_copy = beside(1, att_mine, att_sib)

    def window(col, hslot, part):
        return kv.at[col, part, tile_of(hslot)]

    def along_height(wslot, part):
        col = own + wslot
        for i, (there, to) in enumerate(neighbours(h)):
            slot = h - start(to)
            yield there, remote(
                window(col, place.hslot, part), window(col, slot, part),
                hsend.at[i, wslot, part], recv.at[col, slot, part], (place.f, to, place.w),
            )

    def along_width(hslot, part):
        for i, (there, to) in enumerate(neighbours(place.w)):
            col = own + place.w - start(to)
            yield there, remote(
                window(own + place.wslot, hslot, part), window(col, hslot, part),
                wsend.at[i, hslot, part], recv.at[col, hslot, part], (place.f, h, to),
            )

    def to_sibling(wslot, hslot, part):
        col = own + wslot
        yield True, remote(
            window(col, hslot, part), window(col, hslot, part), ssend.at[wslot, hslot, part],
            recv.at[col, hslot, part], place.sibling,
        )

    def take(plane, wslot, hslot, part):
        col = plane + wslot
        arrived(window(col, hslot, part), recv.at[col, hslot, part])

    def forward(plane, base, first, tiles, prob, prob_grad, col_max, state, total):
        rows = [tile_of(hslot) for _, hslot in tiles]
        scores = [
            dot(kv[plane + wslot, 0, row], queries[first : first + WIDE], (1, 1))
            for (wslot, _), row in zip(tiles, rows)
        ]
        before = state[0:1]
        now = before
        for score in scores:
            now = jnp.maximum(now, jnp.max(score, axis=0, keepdims=True))
        shrink = jnp.exp2((before - now) * SCALE)
        row_sum = state[1:2] * shrink
        added = jnp.zeros((DIM, WIDE), F32)
        for (wslot, hslot), row, score in zip(tiles, rows, scores):
            weights = jnp.exp2((score - now) * SCALE)
            row_sum += jnp.sum(weights, axis=0, keepdims=True)
            values = kv[plane + wslot, 1, row]
            prob[base + wslot, row] = weights
            prob_grad[base + wslot, row] = dot(values, douts[first : first + WIDE], (1, 1))
            col_max[base + wslot, hslot] = now
            added += dot(values, weights.astype(BF16), (0, 0))
        state[0:1] = now
        state[1:2] = row_sum
        total[...] = total[...] * shrink + added

    def ours(plane, tiles):
        forward(plane, plane, 0, tiles, own_prob, own_grad, own_max, own_state, own_att)

    def theirs(tiles):
        forward(
            lent, 0, WIDE, tiles, their_prob, their_grad, their_max, their_state, their_att
        )

    def from_sibling(tiles):
        for wslot, hslot in tiles:
            for part in range(2):
                take(sib, wslot, hslot, part)

    w0, h0 = wslots[0], hslots[0]
    begin(along_height(w0, 0))
    begin(along_width(h0, 1))
    begin(along_width(h0, 0))
    begin(along_height(w0, 1))
    begin(to_sibling(w0, h0, 0))
    begin(to_sibling(w0, h0, 1))
    query_copy.start()
    dout_copy.start()
    grads_copy.start()
    for wslot, hslot in zip(wslots[1:], hslots[1:]):
        take(own, w0, hslot, 0)
        begin(along_width(hslot, 0))
        begin(to_sibling(w0, hslot, 0))
        take(own, wslot, h0, 1)
        begin(along_height(wslot, 1))
        begin(to_sibling(wslot, h0, 1))
    for wslot, hslot in zip(wslots[1:], hslots[1:]):
        take(own, w0, hslot, 1)
        begin(to_sibling(w0, hslot, 1))
        take(own, wslot, h0, 0)
        begin(to_sibling(wslot, h0, 0))
    steps = [[(w0, hslot) for hslot in hslots]]
    steps += [[(wslot, hslot) for wslot in wslots[1:]] for hslot in hslots]

    def from_corners(tiles):
        for part in range(2):
            for wslot, hslot in tiles:
                take(own, wslot, hslot, part)
                begin(to_sibling(wslot, hslot, part))

    ours(own, steps[0])
    query_copy.wait()
    dout_copy.wait()
    from_sibling(steps[0])
    theirs(steps[0])
    ours(sib, steps[0])
    ours(own, steps[1])
    from_sibling(steps[1])
    theirs(steps[1])
    ours(sib, steps[1])
    from_corners(steps[2])
    ours(own, steps[2])
    from_corners(steps[3])
    from_sibling(steps[2])
    theirs(steps[2])
    ours(sib, steps[2])
    ours(own, steps[3])
    from_sibling(steps[3])
    theirs(steps[3])
    att_out[...] = their_att[...].astype(BF16)
    att_copy.start()
    state_copy.start()
    ours(sib, steps[3])

    grads_copy.wait()
    att_copy.wait()
    state_copy.wait()
    before = own_state[0:1]
    row_max = jnp.maximum(before, state_in[0:1])
    shrink = jnp.exp2((before - row_max) * SCALE)
    shrink_in = jnp.exp2((state_in[0:1] - row_max) * SCALE)
    inverse = 1.0 / (own_state[1:2] * shrink + state_in[1:2] * shrink_in)
    attended_wide = (
        (own_att[...] * shrink + att_in[...].astype(F32) * shrink_in) * inverse
    ).astype(BF16)
    att_mine[...] = attended_wide
    sib_copy.start()
    attended = attended_wide[:, :ROWS]
    stats_out[0:1] = row_max
    stats_out[1:2] = inverse
    stats_out[2:3] = jnp.sum(
        jnp.transpose(douts[:WIDE].astype(F32)) * attended_wide.astype(F32), axis=0, keepdims=True
    )
    stats_copy.start()
    for i in range(3):
        columns = pl.ds(pl.multiple_of(core * 1536 + i * 512, 512), 512)
        terms[i] = dot(attended, grads[:, columns], (1, 0))
    sib_copy.wait()
    for i in range(3):
        term = terms[i] + dot(
            att_sib[:, :ROWS], grads_in[:, i * 512 : (i + 1) * 512], (1, 0)
        )
        for j in range(4):
            half[i * 512 + j * 128 : i * 512 + (j + 1) * 128] = term[
                :, j * 128 : (j + 1) * 128
            ].astype(BF16)

    def backward(plane, wslot, both):
        added = jnp.zeros((DIM, 2 * WIDE if both else WIDE), F32)
        for hslot in range(3):
            rows = tile_of(hslot)
            held = [(own_prob, own_grad, own_max, stats_out, plane + wslot)]
            if both:
                held.append((their_prob, their_grad, their_max, stats_in, wslot))
            shares, score_grads = [], []
            for prob, prob_grad, col_max, stats, col in held:
                share = jnp.exp2((col_max[col, hslot] - stats[0:1]) * SCALE) * stats[1:2]
                probability = prob[col, rows] * share
                shares.append(probability.astype(BF16))
                score_grads.append(
                    (probability * (prob_grad[col, rows] - stats[2:3])).astype(BF16)
                )
            share = jnp.concatenate(shares, axis=1) if both else shares[0]
            score_grad = jnp.concatenate(score_grads, axis=1) if both else score_grads[0]
            width = added.shape[1]
            value_part = dot(share, douts[:width], (1, 0))
            key_part = dot(score_grad, queries[:width], (1, 0)) * ROOT
            parts[plane + wslot, 1, rows] = value_part.astype(BF16)
            parts[plane + wslot, 0, rows] = key_part.astype(BF16)
            added += dot(kv[plane + wslot, 0, rows], score_grad, (0, 0))
        dquery[:, : added.shape[1]] += added

    def swap_copy(wslot):
        return remote(
            parts.at[sib + wslot], swap.at[wslot], swap_send.at[wslot], swap_recv.at[wslot],
            place.sibling,
        )

    def own_column(wslot, carry):
        backward(kept, wslot, False)
        pl.when(place.lends_own)(swap_copy(wslot).start)
        return carry

    def piece_copy(chunk, k):
        to = place.plane_shift(k)
        return remote(
            half.at[piece_of(to, chunk)], pieces.at[chunk, ring], piece_send.at[chunk, to],
            piece_recv.at[chunk, ring], place.plane_chip(k),
        )

    for chunk in range(CHUNKS):

        for k in FAR_FIRST:
            piece_copy(chunk, k).start()
    lax.fori_loop(0, 3, own_column, 0)
    stats_copy.wait()

    def lent_column(wslot, carry):
        backward(lent, wslot, True)
        pl.when(place.lends_sib)(swap_copy(wslot).start)
        return carry

    lax.fori_loop(0, 3, lent_column, 0)
    dquery_out[...] = dquery[:, WIDE:]
    dquery_copy.start()

    def own_tile(wslot, hslot):
        rows = tile_of(hslot)
        outgoing[wslot, :, rows] = parts[own + wslot, :, rows].astype(F32) + swap[
            wslot, :, rows
        ].astype(F32)
        swap[wslot, :, rows] = outgoing[wslot, :, rows].astype(BF16)

    back = (1, 0, 2)

    def width_copy(i, to, hslot):
        return remote(
            swap.at[to - start(place.w), 0, tile_of(hslot)], wide.at[back[i], hslot],
            wide_send.at[i, hslot], wide_recv.at[back[i], hslot], (place.f, h, to),
        )

    def tall_copy(i, to, wslot):
        return remote(
            swap.at[wslot, 1, tile_of(to - start(h))], tall.at[back[i], wslot],
            tall_send.at[i, wslot], tall_recv.at[back[i], wslot], (place.f, to, place.w),
        )

    def own_rows(wslot, carry):
        arrived(swap.at[wslot], swap_recv.at[wslot])
        for hslot in range(3):
            own_tile(wslot, hslot)
        return carry

    lax.fori_loop(0, 3, own_rows, 0)

    def three(body):
        def one(slot, carry):
            body(slot)
            return carry

        lax.fori_loop(0, 3, one, 0)

    for i, (there, to) in enumerate(owners(place.w)):
        pl.when(there)(lambda: three(lambda slot: width_copy(i, to, slot).start()))
    for i, (there, to) in enumerate(owners(h)):
        pl.when(there)(lambda: three(lambda slot: tall_copy(i, to, slot).start()))

    def project(i, carry):
        columns = pl.ds(pl.multiple_of(i * 512, 512), 512)
        projected[:, columns] = dot(attended, weight[:, columns], (0, 0)).astype(BF16)
        return carry

    lax.fori_loop(0, 6, project, 0)
    store = pltpu.make_async_copy(projected, projected_hbm, store_sem.at[0])
    store.start()
    def line_copy(chunk, k):
        to = place.hs[k]
        return remote(
            lines.at[chunk, h], lines.at[chunk, h], line_send.at[chunk, to],
            line_recv.at[chunk, h], (place.f, to, place.w),
        )

    def exchange(chunk):
        total = half[piece_of(ring, chunk)].astype(F32)
        for k in range(1, 16):
            other = place.plane_shift(k)
            arrived(pieces.at[chunk, other], piece_recv.at[chunk, other])
            total = total + pieces[chunk, other].astype(F32)
        lines[chunk, h] = total.astype(BF16)
        for k in (4, 3, 5, 2, 6, 1, 7):
            line_copy(chunk, k).start()
        return total

    totals = [exchange(chunk) for chunk in range(CHUNKS)]

    def full_copy(chunk, k):
        to = place.plane_shift(k)
        rows = piece_of(ring, chunk)
        return remote(
            full.at[core, rows], full.at[core, rows], full_send.at[chunk, to],
            full_recv.at[chunk, ring], place.plane_chip(k),
        )

    def pass_copy(chunk, group):
        rows = group_of(group, chunk)
        return remote(
            full.at[core, rows], full.at[core, rows], pass_send.at[chunk, group],
            pass_recv.at[chunk, group], place.sibling,
        )

    def spread(chunk):
        total = totals[chunk]
        for k in range(1, 8):
            other = place.hs[k]
            arrived(lines.at[chunk, other], line_recv.at[chunk, other])
            total = total + lines[chunk, other].astype(F32)
        full[core, piece_of(ring, chunk)] = (total * (1.0 / 256.0)).astype(BF16)
        for k in FAR_FIRST:
            full_copy(chunk, k).start()

    spread(0)

    def add_wide(i, hslot):
        arrived(wide.at[i, hslot], wide_recv.at[i, hslot])
        outgoing[place.wslot, 0, tile_of(hslot)] += wide[i, hslot].astype(F32)

    def add_tall(i, wslot):
        arrived(tall.at[i, wslot], tall_recv.at[i, wslot])
        outgoing[wslot, 1, tile_of(place.hslot)] += tall[i, wslot].astype(F32)

    for i, (there, _w) in enumerate(neighbours(place.w)):
        pl.when(there)(lambda: three(lambda slot: add_wide(i, slot)))
    for i, (there, _h) in enumerate(neighbours(h)):
        pl.when(there)(lambda: three(lambda slot: add_tall(i, slot)))

    def height_copy(i, to):
        rows = tile_of(to - start(h))
        return remote(
            swap.at[place.wslot, 0, rows], high.at[back[i]], high_send.at[i],
            high_recv.at[back[i]], (place.f, to, place.w),
        )

    def side_copy(i, to):
        rows = tile_of(place.hslot)
        return remote(
            swap.at[to - start(place.w), 1, rows], side.at[back[i]], side_send.at[i],
            side_recv.at[back[i]], (place.f, h, to),
        )

    for i, (there, to) in enumerate(owners(h)):

        @pl.when(there)
        def _():
            rows = tile_of(to - start(h))
            swap[place.wslot, 0, rows] = outgoing[place.wslot, 0, rows].astype(BF16)
            height_copy(i, to).start()

    for i, (there, to) in enumerate(owners(place.w)):

        @pl.when(there)
        def _():
            rows = tile_of(place.hslot)
            wslot = to - start(place.w)
            swap[wslot, 1, rows] = outgoing[wslot, 1, rows].astype(BF16)
            side_copy(i, to).start()

    for chunk in range(1, CHUNKS):
        spread(chunk)
    dquery_copy.wait()
    query_out[...] = (jnp.transpose(dquery[:, :WIDE] + dquery_in[...])[:ROWS] * ROOT).astype(BF16)


    for chunk in range(CHUNKS):
        for k in range(1, 16):
            piece_copy(chunk, k).wait_send()
        for k in range(1, 8):
            line_copy(chunk, k).wait_send()

    def left_column(slot, carry):
        swap_copy(slot).wait_send()
        for hslot in range(3):
            for part in range(2):
                finish(to_sibling(slot, hslot, part))
        finish(along_width(slot, 0))
        finish(along_height(slot, 1))
        return carry

    lax.fori_loop(0, 3, left_column, 0)
    finish(along_height(w0, 0))
    finish(along_width(h0, 1))
    for i, (there, to) in enumerate(owners(place.w)):
        pl.when(there)(lambda: three(lambda slot: width_copy(i, to, slot).wait_send()))
    for i, (there, to) in enumerate(owners(h)):
        pl.when(there)(lambda: three(lambda slot: tall_copy(i, to, slot).wait_send()))

    rows = tile_of(place.hslot)
    for i, (there, _h) in enumerate(neighbours(h)):

        @pl.when(there)
        def _():
            arrived(high.at[i], high_recv.at[i])
            outgoing[place.wslot, 0, rows] += high[i].astype(F32)

    for i, (there, _w) in enumerate(neighbours(place.w)):

        @pl.when(there)
        def _():
            arrived(side.at[i], side_recv.at[i])
            outgoing[place.wslot, 1, rows] += side[i].astype(F32)

    kv_out[...] = outgoing[place.wslot, :, rows].astype(BF16)

    for chunk in range(CHUNKS):

        for group in range(4):
            for k in range(4 * group, 4 * group + 4):
                if k:
                    other = place.plane_shift(k)
                    arrived(full.at[core, piece_of(other, chunk)], full_recv.at[chunk, other])
            pass_copy(chunk, place.xs[group]).start()
    store_half = pltpu.make_async_copy(full.at[core], full_hbm.at[core], store_sem.at[1])
    store_half.start()

    for chunk in range(CHUNKS):
        for group in range(4):
            arrived(full.at[1 - core, group_of(group, chunk)], pass_recv.at[chunk, group])
    store_rest = pltpu.make_async_copy(
        full.at[1 - core], full_hbm.at[1 - core], store_sem.at[2]
    )
    store_rest.start()

    for chunk in range(CHUNKS):
        for k in range(1, 16):
            full_copy(chunk, k).wait_send()

    for chunk in range(CHUNKS):
        for group in range(4):
            pass_copy(chunk, group).wait_send()
    for i, (there, to) in enumerate(owners(place.w)):
        pl.when(there)(side_copy(i, to).wait_send)
    for i, (there, to) in enumerate(owners(h)):
        pl.when(there)(height_copy(i, to).wait_send)
    store.wait()
    store_half.wait()
    store_rest.wait()


def write_kernel(
    projected, query, kv, full, projected_out, query_out, key_out, value_out, weight_out,
    rows, tiles, held, wide, load_sem, store_sem,
):
    pairs = [
        (full.at[0], held.at[0], None),
        (full.at[1], held.at[1], None),
        (query, tiles.at[0], query_out),
        (kv.at[0], tiles.at[1], key_out),
        (kv.at[1], tiles.at[2], value_out),
    ]
    for i in range(4):
        part = pl.ds(i * 48, 48)
        pairs.append((projected.at[part], rows.at[part], projected_out.at[part]))
    loads = [
        pltpu.make_async_copy(source, here, load_sem.at[i])
        for i, (source, here, _) in enumerate(pairs)
    ]
    for load in loads:
        load.start()
    stores = []
    for i, (_, here, target) in enumerate(pairs):
        loads[i].wait()
        if i < 2:
            for block in range(12):
                wide[i, :, block * 128 : (block + 1) * 128] = held[
                    i, block * 128 : (block + 1) * 128
                ].astype(F32)
            here, target = wide.at[i], weight_out.at[:, i * 1536 : (i + 1) * 1536]
        stores.append(pltpu.make_async_copy(here, target, store_sem.at[i]))
        stores[i].start()
    for store in stores:
        store.wait()


def body(queries, key_vectors, value_vectors, out_weight, projected_grad):
    vmem, dma = pltpu.VMEM, pltpu.SemaphoreType.DMA
    model = out_weight.shape[1]
    column = (2, 3 * ROWS, DIM)
    here, there = pl.BlockSpec(memory_space=pltpu.VMEM), pl.BlockSpec(memory_space=pl.ANY)
    tile = (ROWS, DIM)
    results = pl.pallas_call(
        kernel,
        out_shape=(
            jax.ShapeDtypeStruct((ROWS, model), BF16),
            jax.ShapeDtypeStruct(tile, BF16),
            jax.ShapeDtypeStruct((2, ROWS, DIM), BF16),
            jax.ShapeDtypeStruct((2, 1536, DIM), BF16),
        ),
        in_specs=[here, here, here, there, there],
        out_specs=[there, here, here, there],
        scratch_shapes=[
            vmem((6,) + column, BF16),
            vmem((2 * WIDE, DIM), BF16),
            vmem((2 * WIDE, DIM), BF16),
            vmem((6, 3 * ROWS, WIDE), F32),
            vmem((6, 3 * ROWS, WIDE), F32),
            vmem((6, 3, 1, WIDE), F32),
            vmem((3, 3 * ROWS, WIDE), F32),
            vmem((3, 3 * ROWS, WIDE), F32),
            vmem((3, 3, 1, WIDE), F32),
            vmem((8, WIDE), F32),
            vmem((8, WIDE), F32),
            vmem((DIM, WIDE), F32),
            vmem((DIM, WIDE), F32),
            vmem((DIM, WIDE), BF16),
            vmem((DIM, WIDE), BF16),
            vmem((8, WIDE), F32),
            vmem((DIM, WIDE), BF16),
            vmem((DIM, WIDE), BF16),
            vmem((8, WIDE), F32),
            vmem((8, WIDE), F32),
            vmem((DIM, 2 * WIDE), F32),
            vmem((DIM, WIDE), F32),
            vmem((DIM, WIDE), F32),
            vmem((ROWS, model), BF16),
            vmem((ROWS, 1536), BF16),
            vmem((DIM, model), BF16),
            vmem((ROWS, model), BF16),
            vmem((3, DIM, 512), F32),
            vmem((1536, DIM), BF16),
            vmem((CHUNKS, 16, CHUNK, DIM), BF16),
            vmem((CHUNKS, 8, CHUNK, DIM), BF16),
            vmem((2, 1536, DIM), BF16),
            vmem((6,) + column, BF16),
            vmem((3,) + column, BF16),
            vmem((3,) + column, F32),
            vmem((3, 3) + tile, BF16),
            vmem((3, 3) + tile, BF16),
            vmem((3,) + tile, BF16),
            vmem((3,) + tile, BF16),
            dma((2,)),
            dma((3,)),
            dma((3, 3, 2)),
            dma((3, 3, 2)),
            dma((3, 3, 2)),
            dma((6, 3, 2)),
            dma((6,)),
            dma((6,)),
            dma((4,)),
            dma((CHUNKS, 16)),
            dma((CHUNKS, 16)),
            dma((CHUNKS, 8)),
            dma((CHUNKS, 8)),
            dma((CHUNKS, 16)),
            dma((CHUNKS, 4)),
            dma((CHUNKS, 4)),
            dma((CHUNKS, 16)),
            dma((3,)),
            dma((3,)),
            dma((3, 3)),
            dma((3, 3)),
            dma((3, 3)),
            dma((3, 3)),
            dma((3,)),
            dma((3,)),
            dma((3,)),
            dma((3,)),
        ],
        compiler_params=pltpu.CompilerParams(
            collective_id=0, has_side_effects=True, vmem_limit_bytes=LIMIT
        ),
        name="attention",
    )(
        queries.reshape(tile),
        key_vectors.reshape(tile),
        value_vectors.reshape(tile),
        out_weight,
        projected_grad.reshape(ROWS, model),
    )
    projected, grad_query, grad_key, grad_value, grad_out_weight = pl.pallas_call(
        write_kernel,
        out_shape=(
            jax.ShapeDtypeStruct((ROWS, model), BF16),
            jax.ShapeDtypeStruct(tile, BF16),
            jax.ShapeDtypeStruct(tile, BF16),
            jax.ShapeDtypeStruct(tile, BF16),
            jax.ShapeDtypeStruct((DIM, model), F32),
        ),
        in_specs=[there] * 4,
        out_specs=[there] * 5,
        scratch_shapes=[
            vmem((ROWS, model), BF16),
            vmem((3,) + tile, BF16),
            vmem((2, 1536, DIM), BF16),
            vmem((2, DIM, 1536), F32),
            dma((9,)),
            dma((9,)),
        ],
        compiler_params=pltpu.CompilerParams(vmem_limit_bytes=LIMIT),
        name="write",
    )(*results)
    return (
        projected.reshape(projected_grad.shape),
        grad_query.reshape(queries.shape),
        grad_key.reshape(queries.shape),
        grad_value.reshape(queries.shape),
        grad_out_weight,
    )


def solution(mesh):
    spec = P("frame", "height", "width", None)
    return jax.shard_map(
        body,
        mesh=mesh,
        in_specs=(spec, spec, spec, P(), spec),
        out_specs=(spec, spec, spec, spec, P()),
        check_vma=False,
    )
```
